256 devices in a mesh: row: 16 (over z, core), col: 8 (over y_hi, x), rep: 2 (over y_lo).
Axes of the slice: x: 4, y: 4 (y_hi: 2, y_lo: 2; y = y_hi * 2 + y_lo), z: 8, core: 2. Of those that a mesh axis runs over, the one named last changes fastest.
Arguments:
- node_features: bfloat16 [65536, 256], P(('row', 'col', 'rep')), may hold values from -6 to 6
- weight: bfloat16 [256, 256], replicated, may hold values from -0.375 to 0.375
- cotangent: bfloat16 [65536, 256], P(('col', 'rep', 'row')), may hold values from -6 to 6
- adjacency_blocks: bfloat16 [16, 16, 256, 128, 128], P(('col', 'rep'), 'row'), may hold values from -0.0625 to 0.0625
- block_coords: int32 [16, 16, 2, 256], P(('col', 'rep'), 'row'), may hold values from 0 to 31, as said below
- block_counts: int32 [16, 16], P(('col', 'rep'), 'row'), may hold values from 1 to 256, as said below
Outputs:
- hidden: bfloat16 [65536, 256], P(('col', 'rep', 'row'))
- weight_grad: float32 [256, 256], replicated
- feature_grad: bfloat16 [65536, 256], P(('row', 'col', 'rep'))
The draws below stay inside these ranges and needn't reach their ends.
Inputs may be any that keep to these rules, and one draw needn't show every extreme that they name: block_coords[i, r, 0, k] is a block row below 32 and block_coords[i, r, 1, k] a block column below 32; within a tile the first min(256, 1024) slots name distinct positions. Only the first block_counts[i, r] slots of tile (i, r) belong to the adjacency; the values and coordinates in its other slots are not part of it.
All inputs are finite; a program needn't handle non-finite values.
Results may differ from the reference program's by a relative error of at most 0.029.
Values may be sent and summed in bfloat16 or wider, within the bound.
No kernel may reach another device: no remote copies, remote signals or barrier semaphores. Data moves between devices by JAX's collectives and lax.ppermute only.
A program may use at most 128 MiB of HBM per device.

```python
import math
import jax
import jax.numpy as jnp
from jax import lax

F = 256
BLK = 128
NODE_DEV = 256
CAP = 256
ROW_TILES = 16
COL_TILES = 16
TILE_ROWS = 4096
TILE_COLS = 4096
ROW_BLOCKS = 32
COL_BLOCKS = 32
NODES = 65536
N_ROW = 16
N_COL = 8
N_REP = 2


def draw_block_coords(key, part):
    positions = ROW_BLOCKS * COL_BLOCKS
    tiles = N_COL * N_REP * N_ROW
    repeats = -(-CAP // positions)

    def one_tile(tile_key):
        inner = jax.random.permutation(tile_key, positions - 2).astype(jnp.int32) + 1
        order = jnp.concatenate([jnp.array([positions - 1, 0], jnp.int32), inner])
        order = jnp.tile(order, repeats)[:CAP]
        return jnp.stack([order // COL_BLOCKS, order % COL_BLOCKS])
    keys = jax.random.split(jax.random.fold_in(key, 11), tiles)
    coords = jax.vmap(one_tile)(keys)
    return coords.reshape(N_COL * N_REP, N_ROW, 2, CAP).astype(jnp.int32)


def draw_block_counts(key, part):
    tiles = N_COL * N_REP * N_ROW
    first_key, second_key, third_key = jax.random.split(jax.random.fold_in(key, 7), 3)
    shifts = jax.random.randint(first_key, (tiles,), 0, 4)
    levels = jnp.maximum(jnp.right_shift(jnp.full((tiles,), CAP, jnp.int32), shifts), 1)
    cuts = jax.random.randint(second_key, (tiles,), 0, levels // 2 + 1)
    filled = jnp.maximum(levels - cuts, 1)
    fullest = jax.random.randint(third_key, (), 0, tiles)
    filled = filled.at[fullest].set(CAP)
    return filled.reshape(N_COL * N_REP, N_ROW).astype(jnp.int32)


def block_levels(own_key, shape, shards, least, top_value):
    gain = 1.0
    for position, shards_of in shards:
        draws = jax.random.uniform(jax.random.fold_in(jax.random.fold_in(own_key, 6), position), (shards_of,), jnp.float32, least / len(shards), top_value / len(shards))
        gain = gain * jnp.repeat(jnp.exp(draws), shape[position] // shards_of).reshape((-1,) + (1,) * (len(shape) - 1 - position))
    return gain


def scatter_about(rng, extent, deviation, bound, cuts=(), kind=jnp.bfloat16):
    result = jax.random.normal(rng, extent, jnp.float32) * deviation
    if len(cuts) > 0:
        result = block_levels(rng, extent, cuts, -0.22, 0.18) * result
    return jnp.clip(result, min=-bound, max=bound).astype(kind)


def setup_inputs(seed: int = 0) -> dict:
    key_of = jax.random.split(jax.random.key(seed), 7)
    return {
        "node_features": scatter_about(key_of[0], (NODES, F), 1.0, 6.0, ((0, 256),)),
        "weight": scatter_about(key_of[1], (F, F), F ** -0.5, 0.375),
        "cotangent": scatter_about(key_of[2], (NODES, F), 1.0, 6.0, ((0, 256),)),
        "adjacency_blocks": scatter_about(key_of[3], (ROW_TILES, COL_TILES, CAP, BLK, BLK), (CAP * BLK * BLK // (2 * NODE_DEV)) ** -0.5, 0.0625, ((0, 16), (1, 16))),
        "block_coords": draw_block_coords(jax.random.fold_in(key_of[6], 71), 0),
        "block_counts": draw_block_counts(jax.random.fold_in(key_of[6], 71), 0),
    }


def silu_slope(values):
    sigma = jax.nn.sigmoid(values)
    return sigma * (1.0 + values * (1.0 - sigma))

def tile_product(blocks, coords, filled, source, out_blocks, flipped):
    slot_total = blocks.shape[0]
    block_size = blocks.shape[1]
    feature_width = source.shape[1]
    group_size = math.gcd(slot_total, 64)
    groups = slot_total // group_size
    source_blocks = source.reshape(-1, block_size, feature_width)
    take_index = coords[0] if flipped else coords[1]
    put_index = coords[1] if flipped else coords[0]
    active = (jnp.arange(slot_total, dtype=jnp.int32) < filled).astype(jnp.float32)
    einsum_form = 'kba,kbf->kaf' if flipped else 'kab,kbf->kaf'

    def accumulate(running, pieces):
        block_group, take_group, put_group, active_group = pieces
        gathered = source_blocks[take_group]
        product = jnp.einsum(einsum_form, block_group.astype(jnp.float32), gathered.astype(jnp.float32))
        product = product * active_group[:, None, None]
        return (running + jax.ops.segment_sum(product, put_group, num_segments=out_blocks), None)
    running = jnp.zeros((out_blocks, block_size, feature_width), jnp.float32)
    running, _ = lax.scan(accumulate, running, (blocks.reshape(groups, group_size, block_size, block_size), take_index.reshape(groups, group_size), put_index.reshape(groups, group_size), active.reshape(groups, group_size)))
    return running.reshape(out_blocks * block_size, feature_width)

def rounded(values):
    return lax.optimization_barrier(values.astype(jnp.bfloat16)).astype(jnp.float32)

def reference(node_features, weight, cotangent, adjacency_blocks, block_coords, block_counts):

    def row_panel(panel):

        def accumulate(running, column):
            source = lax.dynamic_slice_in_dim(node_features, column * TILE_COLS, TILE_COLS, 0)
            term = tile_product(adjacency_blocks[panel, column], block_coords[panel, column], block_counts[panel, column], source, ROW_BLOCKS, False)
            return (running + rounded(term), None)
        running, _ = lax.scan(accumulate, jnp.zeros((TILE_ROWS, F), jnp.float32), jnp.arange(COL_TILES, dtype=jnp.int32))
        return running
    summed = lax.map(row_panel, jnp.arange(ROW_TILES, dtype=jnp.int32)).reshape(NODES, F)
    mixed = summed.astype(jnp.bfloat16)
    pre_act = jnp.dot(mixed, weight, preferred_element_type=jnp.float32)
    hidden = jax.nn.silu(pre_act).astype(jnp.bfloat16)
    act_grad = (cotangent.astype(jnp.float32) * silu_slope(pre_act)).astype(jnp.bfloat16)
    weight_grad = jnp.dot(mixed.T, act_grad, preferred_element_type=jnp.float32) / math.sqrt(NODES)
    mixed_grad = jnp.dot(act_grad, weight.T, preferred_element_type=jnp.float32).astype(jnp.bfloat16)

    def col_panel(column):

        def accumulate(running, panel):
            source = lax.dynamic_slice_in_dim(mixed_grad, panel * TILE_ROWS, TILE_ROWS, 0)
            term = tile_product(adjacency_blocks[panel, column], block_coords[panel, column], block_counts[panel, column], source, COL_BLOCKS, True)
            return (running + rounded(term), None)
        running, _ = lax.scan(accumulate, jnp.zeros((TILE_COLS, F), jnp.float32), jnp.arange(ROW_TILES, dtype=jnp.int32))
        return running
    feature_grad = lax.map(col_panel, jnp.arange(COL_TILES, dtype=jnp.int32)).reshape(NODES, F).astype(jnp.bfloat16)
    return (hidden, weight_grad, feature_grad)
```

```python
import functools
import math

import jax
import jax.numpy as jnp
from jax import lax
from jax.experimental import pallas as pl
from jax.experimental.pallas import tpu as pltpu
from jax.sharding import Mesh, PartitionSpec as P

BLK = 128
UNROLL = 4
PLANE = ("yh", "x", "yl")
BF16 = jnp.bfloat16
F32 = jnp.float32
VMEM_LIMIT = 48 * 1024 * 1024


def slot_tables_kernel(coords_ref, count_ref, table_ref):
    slots = coords_ref.shape[1]
    coords = jnp.concatenate([coords_ref[...], jnp.zeros((6, slots), jnp.int32)], axis=0).astype(F32)
    columns = jnp.transpose(coords)
    lane = lax.broadcasted_iota(jnp.int32, (slots, slots), 1)
    sublane = lax.broadcasted_iota(jnp.int32, (slots, slots), 0)
    filled = count_ref[0]
    rows = []
    for by in range(2):
        key_lane = jnp.where(lane < filled, jnp.broadcast_to(coords[by : by + 1], (slots, slots)), 99.0)
        key_sub = jnp.where(sublane < filled, jnp.broadcast_to(columns[:, by : by + 1], (slots, slots)), 99.0)
        ahead = (key_lane < key_sub) | ((key_lane == key_sub) & (lane < sublane))
        place = jnp.sum(ahead.astype(F32), axis=1, keepdims=True)
        here = (jnp.broadcast_to(place, (slots, slots)) == lane.astype(F32)).astype(F32)
        other = jnp.broadcast_to(columns[:, 1 - by : 2 - by], (slots, slots))
        rows.append(jnp.sum(here * sublane.astype(F32), axis=0, keepdims=True))
        rows.append(jnp.sum(here * other, axis=0, keepdims=True))
        rows.append(jnp.sum((key_sub < lane.astype(F32)).astype(F32), axis=0, keepdims=True))
    rows.append(jnp.zeros((2, slots), F32))
    table_ref[...] = jnp.concatenate(rows, axis=0).astype(jnp.int32)


def slot_tables(coords, count):
    slots = coords.shape[1]
    return pl.pallas_call(
        slot_tables_kernel,
        out_shape=jax.ShapeDtypeStruct((8, slots), jnp.int32),
        in_specs=[pl.BlockSpec(memory_space=pltpu.VMEM), pl.BlockSpec(memory_space=pltpu.SMEM)],
        out_specs=pl.BlockSpec(memory_space=pltpu.VMEM),
    )(coords, count)


def line_sum(table_ref, base, line, blocks_ref, read_source, width, contract):
    begin = table_ref[base + 2, line]
    end = table_ref[base + 2, line + 1]

    def step(i, running):
        for u in range(UNROLL):
            at = begin + i * UNROLL + u
            inside = at < end
            safe = jnp.minimum(at, end - 1)
            block = blocks_ref[table_ref[base, safe]]
            block = jnp.where(inside, block, jnp.zeros_like(block))
            running += lax.dot_general(
                block,
                read_source(table_ref[base + 1, safe]),
                (((contract,), (0,)), ((), ())),
                preferred_element_type=F32,
            )
        return running

    return lax.fori_loop(
        0, (end - begin + UNROLL - 1) // UNROLL, step, jnp.zeros((BLK, width), F32)
    )


def forward_kernel(depth, table_ref, place_ref, blocks_ref, source_ref, sibling_ref, own_ref):
    width = source_ref.shape[1]
    layer, core = place_ref[0], place_ref[1]

    def read_source(at):
        return source_ref[pl.ds(pl.multiple_of(at * BLK, BLK), BLK), :]

    for out_ref, side in ((sibling_ref, 1 - core), (own_ref, core)):

        @pl.loop(0, 2 * depth)
        def _(i, out_ref=out_ref, side=side):
            target = lax.rem(layer + i // 2, depth)
            line = (target * 2 + side) * 2 + lax.rem(i, 2)
            total = line_sum(table_ref, 0, line, blocks_ref, read_source, width, 1)
            out_ref[pl.ds(pl.multiple_of(i * BLK, BLK), BLK), :] = total.astype(BF16)


def forward_product(table, place, blocks, source, depth):
    rows, width = source.shape
    half = jax.ShapeDtypeStruct((rows // 2, width), BF16)
    return pl.pallas_call(
        functools.partial(forward_kernel, depth),
        out_shape=(half, half),
        in_specs=[pl.BlockSpec(memory_space=pltpu.SMEM)] * 2
        + [pl.BlockSpec(memory_space=pltpu.VMEM)] * 2,
        out_specs=(pl.BlockSpec(memory_space=pltpu.VMEM),) * 2,
        compiler_params=pltpu.CompilerParams(vmem_limit_bytes=VMEM_LIMIT),
    )(table, place, blocks, source)


def backward_kernel(depth, table_ref, place_ref, blocks_ref, own_ref, sibling_ref, tail_ref, out_ref, source_ref):
    rows, width = own_ref.shape
    layer, core = place_ref[0], place_ref[1]
    source_ref[pl.ds(0, rows), :] = own_ref[...]
    source_ref[pl.ds(rows, rows), :] = sibling_ref[...]

    def read_source(line):
        side = jnp.bitwise_and(lax.shift_right_logical(line, 1), 1)
        step = lax.rem(lax.shift_right_logical(line, 2) + depth - layer, depth)
        away = jnp.where(side == core, 0, rows)
        at = away + (step * 2 + jnp.bitwise_and(line, 1)) * BLK
        return source_ref[pl.ds(pl.multiple_of(at, BLK), BLK), :]

    parts, padded = out_ref.shape[0], out_ref.shape[1]
    tail = tail_ref.shape[0]

    @pl.loop(0, parts)
    def _(part):
        for h in range(2):
            total = line_sum(table_ref, 3, part * 2 + h, blocks_ref, read_source, width, 0)
            out_ref[part, pl.ds(h * BLK, BLK), :] = total.astype(BF16)
        out_ref[part, pl.ds(padded - tail, tail), :] = tail_ref[...]


def backward_product(table, place, blocks, own, sibling, tail, depth, parts):
    rows, width = own.shape
    return pl.pallas_call(
        functools.partial(backward_kernel, depth),
        out_shape=jax.ShapeDtypeStruct((parts, 2 * BLK + tail.shape[0], width), BF16),
        in_specs=[pl.BlockSpec(memory_space=pltpu.SMEM)] * 2
        + [pl.BlockSpec(memory_space=pltpu.VMEM)] * 4,
        out_specs=pl.BlockSpec(memory_space=pltpu.VMEM),
        scratch_shapes=[pltpu.VMEM((2 * rows, width), BF16)],
        compiler_params=pltpu.CompilerParams(vmem_limit_bytes=VMEM_LIMIT),
    )(table, place, blocks, own, sibling, tail)


def dense_kernel(mine_ref, sibling_ref, up_ref, down_ref, weight_ref, cotangent_ref, hidden_ref, grad_ref, part_ref):
    summed = (mine_ref[...].astype(F32) + sibling_ref[...].astype(F32)) + (
        up_ref[...].astype(F32) + down_ref[...].astype(F32)
    )
    mixed = summed.astype(BF16)
    weight = weight_ref[...]
    pre_act = jnp.dot(mixed, weight, preferred_element_type=F32)
    sigma = jax.nn.sigmoid(pre_act)
    hidden_ref[...] = (pre_act * sigma).astype(BF16)
    slope = sigma * (1.0 + pre_act * (1.0 - sigma))
    act_grad = (cotangent_ref[...].astype(F32) * slope).astype(BF16)
    grad_ref[...] = lax.dot_general(
        act_grad, weight, (((1,), (1,)), ((), ())), preferred_element_type=F32
    ).astype(BF16)
    part_ref[...] = lax.dot_general(
        mixed, act_grad, (((0,), (0,)), ((), ())), preferred_element_type=F32
    )


def dense(mine, sibling, up, down, weight, cotangent):
    shape = cotangent.shape
    return pl.pallas_call(
        dense_kernel,
        out_shape=(
            jax.ShapeDtypeStruct(shape, BF16),
            jax.ShapeDtypeStruct(shape, BF16),
            jax.ShapeDtypeStruct(weight.shape, F32),
        ),
    )(mine, sibling, up, down, weight, cotangent)


def body(sizes, node_features, weight, cotangent, adjacency_blocks, block_coords, block_counts):
    depth, nx, ny = sizes
    plane = nx * ny
    blocks = adjacency_blocks[0, 0]
    local, width = node_features.shape
    node_total = local * plane * depth * 2
    layer = lax.axis_index("z")
    core = lax.axis_index("c")
    place = jnp.stack([layer, core]).astype(jnp.int32)
    across = [(0, 1), (1, 0)]

    def around(shift):
        return [(i, (i + shift) % depth) for i in range(depth)]

    def rank(x, y):
        return ((y % ny) // 2 * nx + x % nx) * 2 + y % 2

    def along(dx, dy):
        return [(rank(x, y), rank(x + dx, y + dy)) for x in range(nx) for y in range(ny)]

    table = slot_tables(block_coords[0, 0], block_counts.reshape(1))
    spread = jnp.broadcast_to(node_features[None], (plane, local, width))
    column_feats = lax.all_to_all(spread, PLANE, 0, 0, tiled=True).reshape(plane * local, width)

    for_sibling, own = forward_product(table, place, blocks, column_feats, depth)
    sibling = lax.ppermute(for_sibling, "c", across)
    own = own.reshape(depth, local, width)
    sibling = sibling.reshape(depth, local, width)

    def term(step):
        return own[step].astype(F32) + sibling[step].astype(F32)

    half = local // 2
    middle = depth // 2
    far = term(middle).astype(BF16)
    up = lax.ppermute(far[:half], "z", around(1))
    down = lax.ppermute(far[half:], "z", around(-1))
    up = jnp.concatenate([up, jnp.zeros_like(up)], axis=0)
    down = jnp.concatenate([jnp.zeros_like(down), down], axis=0)
    for step in range(middle - 1, 0, -1):
        up = lax.ppermute((term(step) + up.astype(F32)).astype(BF16), "z", around(1))
        down = lax.ppermute((term(depth - step) + down.astype(F32)).astype(BF16), "z", around(-1))

    hidden, mixed_grad, weight_part = dense(own[0], sibling[0], up, down, weight, cotangent)

    chunks = {0: mixed_grad}
    ahead = behind = mixed_grad
    for step in range(1, middle):
        ahead = lax.ppermute(ahead, "z", around(1))
        behind = lax.ppermute(behind, "z", around(-1))
        chunks[depth - step] = ahead
        chunks[step] = behind
    chunks[middle] = jnp.concatenate(
        [
            lax.ppermute(ahead[:half], "z", around(1)),
            lax.ppermute(behind[half:], "z", around(-1)),
        ],
        axis=0,
    )
    own_panel = jnp.concatenate([chunks[step] for step in range(depth)], axis=0)
    sibling_panel = lax.ppermute(own_panel, "c", across)

    at_x = lax.axis_index("x")
    at_y = lax.axis_index("yh") * 2 + lax.axis_index("yl")
    for at, size, shift in ((at_x, nx, lambda d: along(d, 0)), (at_y, ny, lambda d: along(0, d))):
        shares = weight_part.reshape(size, -1, width)

        def share(d, shares=shares, at=at, size=size):
            return lax.dynamic_index_in_dim(shares, lax.rem(at + d, size), 0, keepdims=False)

        weight_part = share(0)
        for d in range(1, size):
            weight_part += lax.ppermute(share(d), PLANE, shift(d))
    weight_part += lax.ppermute(weight_part, "c", across)
    hop = 1
    while hop < depth:
        weight_part += lax.ppermute(weight_part, "z", [(i, i ^ hop) for i in range(depth)])
        hop *= 2
    tail = weight_part.astype(BF16)

    back = backward_product(table, place, blocks, own_panel, sibling_panel, tail, depth, plane)
    arrived = lax.all_to_all(back, PLANE, 0, 0, tiled=True)
    feature_grad = jnp.sum(arrived[:, :local].astype(F32), axis=0).astype(BF16)
    gathered = arrived[:, local:].reshape(ny // 2, nx, 2, -1, width)
    weight_sum = gathered.transpose(1, 0, 2, 3, 4).reshape(weight.shape)
    weight_grad = weight_sum.astype(F32) / math.sqrt(node_total)
    return (hidden, weight_grad, feature_grad)


def solution(mesh):
    depth = mesh.shape["row"] // 2
    nx = mesh.shape["col"] // 2
    ny = mesh.shape["rep"] * 2
    fine = Mesh(mesh.devices.reshape(depth, 2, ny // 2, nx, 2), ("z", "c", "yh", "x", "yl"))
    row, col = ("z", "c"), ("yh", "x")
    in_specs = (
        P((*row, *PLANE), None),
        P(),
        P((*PLANE, *row), None),
        P(PLANE, row, None, None, None),
        P(PLANE, row, None, None),
        P(PLANE, row),
    )
    out_specs = (P((*PLANE, *row), None), P(), P((*row, *PLANE), None))
    return jax.shard_map(
        functools.partial(body, (depth, nx, ny)),
        mesh=fine,
        in_specs=in_specs,
        out_specs=out_specs,
        check_vma=False,
    )
```

```python
import functools
import math

import jax
import jax.numpy as jnp
from jax import lax
from jax.experimental import pallas as pl
from jax.experimental.pallas import tpu as pltpu
from jax.sharding import Mesh, PartitionSpec as P

BLK = 128
QUAD = 4
QUADS_A_STEP = 4
PARTS = 8
TABLE = 384
PLANE = ("yh", "x", "yl")
BF16 = jnp.bfloat16
F32 = jnp.float32
VMEM_LIMIT = 24 * 1024 * 1024
SMALL_LIMIT = 8 * 1024 * 1024
VMEM = pl.BlockSpec(memory_space=pltpu.VMEM)
SMEM = pl.BlockSpec(memory_space=pltpu.SMEM)


def slot_tables_kernel(sizes, coords_ref, count_ref, place_ref, table_ref):
    depth, nx, ny = sizes
    slots = coords_ref.shape[1]
    at_z, at_c, at_x, at_y = (place_ref[i] for i in range(4))
    row = coords_ref[0:1, :]
    col = coords_ref[1:2, :]
    away = jnp.bitwise_and((row >> 2) - at_z, depth - 1)
    line_row = jnp.where(jnp.bitwise_and(row >> 1, 1) == at_c, 2 * depth, 0) + away * 2 + jnp.bitwise_and(row, 1)
    rank = col >> 1
    col_x = jnp.bitwise_and(rank >> 1, nx - 1)
    col_y = rank // (2 * nx) * 2 + jnp.bitwise_and(rank, 1)
    off_x = jnp.bitwise_and(col_x - at_x, nx - 1)
    off_y = jnp.bitwise_and(col_y - at_y, ny - 1)
    line_col = (off_y * nx + off_x) * 2 + jnp.bitwise_and(col, 1)
    lines = jnp.concatenate([line_row, line_col, jnp.zeros((6, slots), jnp.int32)], axis=0).astype(F32)
    columns = jnp.transpose(lines)
    filled = count_ref[0]

    def iota(width, axis):
        return lax.broadcasted_iota(jnp.int32, (slots, width), axis)

    lane, sublane = iota(slots, 1), iota(slots, 0)
    rows = []
    for by in range(2):
        key = jnp.where(iota(1, 0) < filled, columns[:, by : by + 1], 99.0)
        key_lane = jnp.where(lane < filled, jnp.broadcast_to(lines[by : by + 1], (slots, slots)), 99.0)
        key_sub = jnp.broadcast_to(key, (slots, slots))
        ahead = (key_lane == key_sub) & (lane < sublane)
        order = jnp.sum(ahead.astype(F32), axis=1, keepdims=True)
        spot = iota(BLK, 1).astype(F32)
        key_spot = jnp.broadcast_to(key, (slots, BLK))
        held = jnp.sum((key_spot == spot).astype(F32), axis=0, keepdims=True)
        quads = jnp.where(spot[:1] < 99.0, jnp.floor((held + (QUAD - 1)) * (1.0 / QUAD)), 0.0)
        before = jnp.where(spot < key_spot, jnp.broadcast_to(quads, (slots, BLK)), 0.0)
        entry = jnp.sum(before, axis=1, keepdims=True) * QUAD + order
        target = iota(TABLE, 1).astype(F32)
        active = iota(TABLE, 0) < filled
        here = (jnp.broadcast_to(entry, (slots, TABLE)) == target) & active

        def placed(value):
            return jnp.sum(jnp.where(here, jnp.broadcast_to(value, (slots, TABLE)), 0.0), axis=0, keepdims=True)

        rows.append(placed(iota(1, 0).astype(F32) + 1.0))
        rows.append(placed(columns[:, 1 - by : 2 - by]))
        rows.append(placed(columns[:, by : by + 1]))
        whole = jnp.sum(quads, axis=1, keepdims=True)
        first = jnp.sum(jnp.where(spot[:1] < 2 * depth, quads, 0.0), axis=1, keepdims=True)
        which = lax.broadcasted_iota(jnp.int32, (1, TABLE), 1)
        rows.append(jnp.where(which == 0, jnp.broadcast_to(whole, (1, TABLE)), jnp.broadcast_to(first, (1, TABLE))))
    table_ref[...] = jnp.concatenate(rows, axis=0).astype(jnp.int32)


def slot_tables(coords, count, place, sizes):
    return pl.pallas_call(
        functools.partial(slot_tables_kernel, sizes),
        out_shape=jax.ShapeDtypeStruct((8, TABLE), jnp.int32),
        in_specs=[VMEM, SMEM, SMEM],
        out_specs=VMEM,
        compiler_params=pltpu.CompilerParams(vmem_limit_bytes=SMALL_LIMIT),
    )(coords, count, place)


def add_quads(table_ref, base, begin, end, first_line, blocks_ref, source_ref, total_ref, contract):
    def quad(at):
        inside = at < end
        parts = []
        for u in range(QUAD):
            tag = table_ref[base, at * QUAD + u]
            block = blocks_ref[jnp.maximum(tag - 1, 0)]
            valid = jnp.logical_and(inside, tag > 0)
            parts.append(
                (jnp.where(valid, block, jnp.zeros_like(block)), source_ref[table_ref[base + 1, at * QUAD + u]])
            )
        product = None
        for u in range(0, QUAD, 2):
            left = jnp.concatenate([parts[u][0], parts[u + 1][0]], axis=contract)
            right = jnp.concatenate([parts[u][1], parts[u + 1][1]], axis=0)
            term = lax.dot_general(left, right, (((contract,), (0,)), ((), ())), preferred_element_type=F32)
            product = term if product is None else product + term
        line = jnp.where(inside, table_ref[base + 2, at * QUAD] - first_line, 0)
        return line, product

    @pl.loop(0, (end - begin + QUADS_A_STEP - 1) // QUADS_A_STEP)
    def _(i):
        found = [quad(begin + i * QUADS_A_STEP + j) for j in range(QUADS_A_STEP)]
        for line, product in found:
            total_ref[line] += product


def forward_kernel(own_half, sizes, table_ref, blocks_ref, *refs):
    depth, nx, ny = sizes
    *piece_refs, out_ref, source_ref, total_ref = refs
    lanes = piece_refs[0].shape[-1]
    for oy in range(ny):
        for ox in range(nx):
            for h in range(2):
                for half, major, minor in ((0, oy, ox), (1, ox, oy)):
                    piece = piece_refs[half * ny + major]
                    source_ref[(oy * nx + ox) * 2 + h, :, half * lanes : (half + 1) * lanes] = piece[
                        pl.ds((minor * 2 + h) * BLK, BLK), :
                    ]
    total_ref[...] = jnp.zeros_like(total_ref)
    whole, first = table_ref[3, 0], table_ref[3, 1]
    begin, end, line = (first, whole, 2 * depth) if own_half else (0, first, 0)
    add_quads(table_ref, 0, begin, end, line, blocks_ref, source_ref, total_ref, 1)
    out_ref[...] = total_ref[...].astype(BF16)


def forward_product(own_half, table, blocks, pieces, sizes):
    depth, nx, ny = sizes
    width = 2 * pieces[0].shape[-1]
    lines = 2 * depth
    return pl.pallas_call(
        functools.partial(forward_kernel, own_half, sizes),
        out_shape=jax.ShapeDtypeStruct((lines, BLK, width), BF16),
        in_specs=[SMEM] + [VMEM] * (1 + len(pieces)),
        out_specs=VMEM,
        scratch_shapes=[
            pltpu.VMEM((nx * ny * 2, BLK, width), BF16),
            pltpu.VMEM((lines, BLK, width), F32),
        ],
        compiler_params=pltpu.CompilerParams(vmem_limit_bytes=VMEM_LIMIT),
    )(table, blocks, *pieces)


def backward_kernel(sizes, table_ref, place_ref, blocks_ref, sibling_ref, own_ref, tail_ref, out_ref, source_ref, total_ref):
    depth, nx, ny = sizes
    source_ref[0 : 2 * depth] = sibling_ref[...]
    source_ref[2 * depth :] = own_ref[...]
    total_ref[...] = jnp.zeros_like(total_ref)
    add_quads(table_ref, 4, 0, table_ref[7, 0], 0, blocks_ref, source_ref, total_ref, 0)
    at_x, at_y = place_ref[2], place_ref[3]
    local = 2 * BLK
    for oy in range(ny):
        for ox in range(nx):
            y = jnp.bitwise_and(at_y + oy, ny - 1)
            rank = (y // 2 * nx + jnp.bitwise_and(at_x + ox, nx - 1)) * 2 + jnp.bitwise_and(y, 1)
            for h in range(2):
                out_ref[rank, h * BLK : (h + 1) * BLK, :] = total_ref[(oy * nx + ox) * 2 + h].astype(BF16)
            out_ref[rank, local:, :] = tail_ref[...]


def backward_product(table, place, blocks, sibling, own, tail, sizes):
    depth, nx, ny = sizes
    lines, _, width = own.shape
    return pl.pallas_call(
        functools.partial(backward_kernel, sizes),
        out_shape=jax.ShapeDtypeStruct((nx * ny, 2 * BLK + tail.shape[0], width), BF16),
        in_specs=[SMEM] * 2 + [VMEM] * 4,
        out_specs=VMEM,
        scratch_shapes=[
            pltpu.VMEM((2 * lines, BLK, width), BF16),
            pltpu.VMEM((nx * ny * 2, BLK, width), F32),
        ],
        compiler_params=pltpu.CompilerParams(vmem_limit_bytes=VMEM_LIMIT),
    )(table, place, blocks, sibling, own, tail)


def hold_kernel(count_ref, blocks_ref, held_ref, sem):
    size = blocks_ref.shape[0] // PARTS
    filled = count_ref[0]

    def part(i):
        at = pl.ds(i * size, size)
        return pltpu.make_async_copy(blocks_ref.at[at], held_ref.at[at], sem.at[i])

    for i in range(PARTS):

        @pl.when(filled > i * size)
        def _(i=i):
            part(i).start()

        @pl.when(filled <= i * size)
        def _(i=i):
            held_ref[pl.ds(i * size, size)] = jnp.zeros((size, *held_ref.shape[1:]), held_ref.dtype)

    for i in range(PARTS):

        @pl.when(filled > i * size)
        def _(i=i):
            part(i).wait()


def hold_blocks(blocks, count):
    return pl.pallas_call(
        hold_kernel,
        out_shape=pltpu.VMEM(blocks.shape, blocks.dtype),
        in_specs=[SMEM, pl.BlockSpec(memory_space=pltpu.MemorySpace.HBM)],
        out_specs=VMEM,
        scratch_shapes=[pltpu.SemaphoreType.DMA((PARTS,))],
        compiler_params=pltpu.CompilerParams(vmem_limit_bytes=VMEM_LIMIT),
    )(count, pltpu.with_memory_space_constraint(blocks, pltpu.MemorySpace.HBM))


def dense_kernel(mixed_ref, weight_ref, cotangent_ref, hidden_ref, grad_ref, part_ref):
    mixed = mixed_ref[...]
    weight = weight_ref[...]
    pre_act = jnp.dot(mixed, weight, preferred_element_type=F32)
    sigma = jax.nn.sigmoid(pre_act)
    hidden_ref[...] = (pre_act * sigma).astype(BF16)
    slope = sigma * (1.0 + pre_act * (1.0 - sigma))
    act_grad = (cotangent_ref[...].astype(F32) * slope).astype(BF16)
    grad_ref[...] = lax.dot_general(
        act_grad, weight, (((1,), (1,)), ((), ())), preferred_element_type=F32
    ).astype(BF16)
    part_ref[...] = lax.dot_general(
        mixed, act_grad, (((0,), (0,)), ((), ())), preferred_element_type=F32
    )


def dense(mixed, weight, cotangent):
    shape = cotangent.shape
    return pl.pallas_call(
        dense_kernel,
        out_shape=(
            jax.ShapeDtypeStruct(shape, BF16),
            jax.ShapeDtypeStruct(shape, BF16),
            jax.ShapeDtypeStruct(weight.shape, F32),
        ),
        compiler_params=pltpu.CompilerParams(vmem_limit_bytes=SMALL_LIMIT),
    )(mixed, weight, cotangent)


def last_sums_kernel(nx, ny, scale, arrived_ref, feature_ref, weight_ref):
    local = feature_ref.shape[0]
    share = arrived_ref.shape[1] - local
    value = arrived_ref[0, 0:local, :].astype(F32)
    for i in range(1, nx * ny):
        value = value + arrived_ref[i, 0:local, :].astype(F32)
    feature_ref[...] = value.astype(BF16)
    for y in range(ny):
        for x in range(nx):
            rank = (y // 2 * nx + x) * 2 + y % 2
            at = (x * ny + y) * share
            weight_ref[at : at + share, :] = arrived_ref[rank, local:, :].astype(F32) * scale


def last_sums(arrived, local, weight_shape, node_total, sizes):
    _, nx, ny = sizes
    return pl.pallas_call(
        functools.partial(last_sums_kernel, nx, ny, 1.0 / math.sqrt(node_total)),
        out_shape=(
            jax.ShapeDtypeStruct((local, weight_shape[1]), BF16),
            jax.ShapeDtypeStruct(weight_shape, F32),
        ),
        in_specs=[VMEM],
        out_specs=(VMEM,) * 2,
        compiler_params=pltpu.CompilerParams(vmem_limit_bytes=VMEM_LIMIT),
    )(arrived)


def body(sizes, node_features, weight, cotangent, adjacency_blocks, block_coords, block_counts):
    depth, nx, ny = sizes
    together = lax.optimization_barrier
    local, width = node_features.shape
    lanes = width // 2
    node_total = local * nx * ny * depth * 2
    at_x = lax.axis_index("x")
    at_y = lax.axis_index("yh") * 2 + lax.axis_index("yl")
    place = jnp.stack([lax.axis_index("z"), lax.axis_index("c"), at_x, at_y]).astype(jnp.int32)
    count = block_counts.reshape(1)

    def rank(x, y):
        return ((y % ny) // 2 * nx + x % nx) * 2 + y % 2

    def send(value, dx, dy):
        pairs = [(rank(x, y), rank(x + dx, y + dy)) for x in range(nx) for y in range(ny)]
        return lax.ppermute(value, PLANE, pairs)

    def climb(value, dz):
        return lax.ppermute(value, "z", [(i, (i + dz) % depth) for i in range(depth)])

    def swap(value, dz=0, core=True):
        pairs = [(z * 2 + c, (z ^ dz) * 2 + (c ^ int(core))) for z in range(depth) for c in range(2)]
        return lax.ppermute(value, ("z", "c"), pairs)

    with jax.named_scope("gather_features"):
        upright, level = node_features[:, :lanes], node_features[:, lanes:]
        got = together(
            tuple(send(upright, -o, 0) for o in range(1, nx)) + tuple(send(level, 0, -o) for o in range(1, ny))
        )
        upright = jnp.concatenate((upright,) + got[: nx - 1], axis=0)
        level = jnp.concatenate((level,) + got[nx - 1 :], axis=0)
        got = together(
            tuple(send(upright, 0, -o) for o in range(1, ny)) + tuple(send(level, -o, 0) for o in range(1, nx))
        )
        pieces = (upright,) + got[: ny - 1] + (level,) + got[ny - 1 :]

    with jax.named_scope("tables"):
        table = slot_tables(block_coords[0, 0], count, place, sizes)
        table, early = together((table, count))
        blocks = hold_blocks(adjacency_blocks[0, 0], early)

    with jax.named_scope("forward"):
        for_sibling = forward_product(False, table, blocks, pieces, sizes)
        sibling = swap(for_sibling)
        own = forward_product(True, table, blocks, pieces, sizes)
        sibling, own = together((sibling, own))
        own = own.reshape(depth, local, width)
        sibling = sibling.reshape(depth, local, width)

    def term(step):
        return own[step].astype(F32) + sibling[step].astype(F32)

    with jax.named_scope("sum_rows"):
        half = local // 2
        middle = depth // 2
        far = term(middle).astype(BF16)
        up, down = together((climb(far[:half], 1), climb(far[half:], -1)))
        up = jnp.concatenate([up, jnp.zeros_like(up)], axis=0)
        down = jnp.concatenate([jnp.zeros_like(down), down], axis=0)
        for step in range(middle - 1, 0, -1):
            up, down = together(
                ((term(step) + up.astype(F32)).astype(BF16), (term(depth - step) + down.astype(F32)).astype(BF16))
            )
            up, down = together((climb(up, 1), climb(down, -1)))
        mixed = (term(0) + (up.astype(F32) + down.astype(F32))).astype(BF16)

    with jax.named_scope("dense"):
        hidden, mixed_grad, weight_part = dense(mixed, weight, cotangent)

    with jax.named_scope("gather_rows"):

        def shares(value, at, size):
            cut = value.reshape(size, -1, width)
            return [lax.dynamic_index_in_dim(cut, lax.rem(at + d, size), 0, keepdims=False) for d in range(size)]

        chunks = {0: mixed_grad}
        ahead = behind = mixed_grad
        part = weight_part
        for step in range(1, middle + 1):
            if step > 1:
                part, ahead, behind = together((part, ahead, behind))
            if step < middle:
                moved = (climb(ahead, 1), climb(behind, -1))
            else:
                moved = (climb(ahead[:half], 1), climb(behind[half:], -1))
            if step == 1:
                cut = shares(part, at_x, nx)
                extra = [send(cut[d], d, 0) for d in range(1, nx)]
                part = cut[0] + (extra[0] + extra[1] + extra[2])
            elif step == 2:
                cut = shares(part, at_y, ny)
                extra = [send(cut[d], 0, d) for d in range(1, ny)]
                part = cut[0] + (extra[0] + extra[1] + extra[2])
            elif step == 3:
                part = part + swap(part)
                part = part + swap(part, 1, False)
            else:
                part = part + swap(part, 2, False)
            ahead, behind = together(moved)
            if step < middle:
                chunks[depth - step] = ahead
                chunks[step] = behind
        chunks[middle] = jnp.concatenate([ahead, behind], axis=0)
        own_panel = jnp.concatenate([chunks[step] for step in range(depth)], axis=0)
        own_panel = own_panel.reshape(2 * depth, BLK, width)
        part, own_panel, late = together((part, own_panel, count))
        sibling_panel = swap(own_panel)
        part = part + swap(part, 4, False)
        blocks = hold_blocks(adjacency_blocks[0, 0], late)
        tail = part.astype(BF16)

    with jax.named_scope("backward"):
        outs = backward_product(table, place, blocks, sibling_panel, own_panel, tail, sizes)

    with jax.named_scope("sum_columns"):
        arrived = lax.all_to_all(outs, PLANE, 0, 0, tiled=True)
        feature_grad, weight_grad = last_sums(arrived, local, weight.shape, node_total, sizes)
    return (hidden, weight_grad, feature_grad)


def solution(mesh):
    depth = mesh.shape["row"] // 2
    nx = mesh.shape["col"] // 2
    ny = mesh.shape["rep"] * 2
    fine = Mesh(mesh.devices.reshape(depth, 2, ny // 2, nx, 2), ("z", "c", "yh", "x", "yl"))
    row = ("z", "c")
    in_specs = (
        P((*row, *PLANE), None),
        P(),
        P((*PLANE, *row), None),
        P(PLANE, row, None, None, None),
        P(PLANE, row, None, None),
        P(PLANE, row),
    )
    out_specs = (P((*PLANE, *row), None), P(), P((*row, *PLANE), None))
    return jax.shard_map(
        functools.partial(body, (depth, nx, ny)),
        mesh=fine,
        in_specs=in_specs,
        out_specs=out_specs,
        check_vma=False,
    )
```

```python
import functools
import math

import jax
import jax.numpy as jnp
from jax import lax
from jax.experimental import pallas as pl
from jax.experimental.pallas import tpu as pltpu
from jax.sharding import Mesh, PartitionSpec as P

BLK = 128
QUAD = 4
QUADS_A_STEP = 8
PARTS = 8
TABLE = 384
PLANE = ("yh", "x", "yl")
BF16 = jnp.bfloat16
F32 = jnp.float32
VMEM_LIMIT = 24 * 1024 * 1024
SMALL_LIMIT = 8 * 1024 * 1024
BESIDE = pl.CostEstimate(flops=4_000_000_000, bytes_accessed=0, transcendentals=0)
VMEM = pl.BlockSpec(memory_space=pltpu.VMEM)
SMEM = pl.BlockSpec(memory_space=pltpu.SMEM)


def slot_tables_kernel(sizes, coords_ref, count_ref, place_ref, table_ref):
    depth, nx, ny = sizes
    slots = coords_ref.shape[1]
    at_z, at_c, at_x, at_y = (place_ref[i] for i in range(4))
    row = coords_ref[0:1, :]
    col = coords_ref[1:2, :]
    away = jnp.bitwise_and((row >> 2) - at_z, depth - 1)
    line_row = jnp.where(jnp.bitwise_and(row >> 1, 1) == at_c, 2 * depth, 0) + away * 2 + jnp.bitwise_and(row, 1)
    rank = col >> 1
    col_x = jnp.bitwise_and(rank >> 1, nx - 1)
    col_y = rank // (2 * nx) * 2 + jnp.bitwise_and(rank, 1)
    off_x = jnp.bitwise_and(col_x - at_x, nx - 1)
    off_y = jnp.bitwise_and(col_y - at_y, ny - 1)
    line_col = (off_y * nx + off_x) * 2 + jnp.bitwise_and(col, 1)
    lines = jnp.concatenate([line_row, line_col, jnp.zeros((6, slots), jnp.int32)], axis=0).astype(F32)
    columns = jnp.transpose(lines)
    filled = count_ref[0]

    def iota(width, axis):
        return lax.broadcasted_iota(jnp.int32, (slots, width), axis)

    lane, sublane = iota(slots, 1), iota(slots, 0)
    rows = []
    for by in range(2):
        key = jnp.where(iota(1, 0) < filled, columns[:, by : by + 1], 99.0)
        key_lane = jnp.where(lane < filled, jnp.broadcast_to(lines[by : by + 1], (slots, slots)), 99.0)
        key_sub = jnp.broadcast_to(key, (slots, slots))
        ahead = (key_lane == key_sub) & (lane < sublane)
        order = jnp.sum(ahead.astype(F32), axis=1, keepdims=True)
        spot = iota(BLK, 1).astype(F32)
        key_spot = jnp.broadcast_to(key, (slots, BLK))
        held = jnp.sum((key_spot == spot).astype(F32), axis=0, keepdims=True)
        quads = jnp.where(spot[:1] < 99.0, jnp.floor((held + (QUAD - 1)) * (1.0 / QUAD)), 0.0)
        before = jnp.where(spot < key_spot, jnp.broadcast_to(quads, (slots, BLK)), 0.0)
        entry = jnp.sum(before, axis=1, keepdims=True) * QUAD + order
        target = iota(TABLE, 1).astype(F32)
        active = iota(TABLE, 0) < filled
        here = (jnp.broadcast_to(entry, (slots, TABLE)) == target) & active

        def placed(value):
            return jnp.sum(jnp.where(here, jnp.broadcast_to(value, (slots, TABLE)), 0.0), axis=0, keepdims=True)

        rows.append(placed(iota(1, 0).astype(F32) + 1.0))
        rows.append(placed(columns[:, 1 - by : 2 - by]))
        rows.append(placed(columns[:, by : by + 1]))
        whole = jnp.sum(quads, axis=1, keepdims=True)
        first = jnp.sum(jnp.where(spot[:1] < 2 * depth, quads, 0.0), axis=1, keepdims=True)
        which = lax.broadcasted_iota(jnp.int32, (1, TABLE), 1)
        rows.append(jnp.where(which == 0, jnp.broadcast_to(whole, (1, TABLE)), jnp.broadcast_to(first, (1, TABLE))))
    table_ref[...] = jnp.concatenate(rows, axis=0).astype(jnp.int32)


def slot_tables(coords, count, place, sizes):
    return pl.pallas_call(
        functools.partial(slot_tables_kernel, sizes),
        out_shape=jax.ShapeDtypeStruct((8, TABLE), jnp.int32),
        in_specs=[VMEM, SMEM, SMEM],
        out_specs=VMEM,
        compiler_params=pltpu.CompilerParams(vmem_limit_bytes=SMALL_LIMIT),
    )(coords, count, place)


def add_quads(table_ref, base, begin, end, first_line, blocks_ref, source_ref, total_ref, contract):
    def quad(at):
        inside = at < end
        parts = []
        for u in range(QUAD):
            tag = table_ref[base, at * QUAD + u]
            block = blocks_ref[jnp.maximum(tag - 1, 0)]
            valid = jnp.logical_and(inside, tag > 0)
            parts.append(
                (jnp.where(valid, block, jnp.zeros_like(block)), source_ref[table_ref[base + 1, at * QUAD + u]])
            )
        product = None
        for u in range(0, QUAD, 2):
            left = jnp.concatenate([parts[u][0], parts[u + 1][0]], axis=contract)
            right = jnp.concatenate([parts[u][1], parts[u + 1][1]], axis=0)
            term = lax.dot_general(left, right, (((contract,), (0,)), ((), ())), preferred_element_type=F32)
            product = term if product is None else product + term
        line = jnp.where(inside, table_ref[base + 2, at * QUAD] - first_line, 0)
        return line, product

    @pl.loop(0, (end - begin + QUADS_A_STEP - 1) // QUADS_A_STEP)
    def _(i):
        found = [quad(begin + i * QUADS_A_STEP + j) for j in range(QUADS_A_STEP)]
        for line, product in found:
            total_ref[line] += product


def forward_kernel(own_half, sizes, table_ref, blocks_ref, *refs):
    depth, nx, ny = sizes
    *piece_refs, out_ref, source_ref, total_ref = refs
    lanes = piece_refs[0].shape[-1]
    for oy in range(ny):
        for ox in range(nx):
            for h in range(2):
                for half, major, minor in ((0, oy, ox), (1, ox, oy)):
                    piece = piece_refs[half * ny + major]
                    source_ref[(oy * nx + ox) * 2 + h, :, half * lanes : (half + 1) * lanes] = piece[
                        pl.ds((minor * 2 + h) * BLK, BLK), :
                    ]
    total_ref[...] = jnp.zeros_like(total_ref)
    whole, first = table_ref[3, 0], table_ref[3, 1]
    begin, end, line = (first, whole, 2 * depth) if own_half else (0, first, 0)
    add_quads(table_ref, 0, begin, end, line, blocks_ref, source_ref, total_ref, 1)
    out_ref[...] = total_ref[...].astype(BF16)


def forward_product(own_half, table, blocks, pieces, sizes):
    depth, nx, ny = sizes
    width = 2 * pieces[0].shape[-1]
    lines = 2 * depth
    return pl.pallas_call(
        functools.partial(forward_kernel, own_half, sizes),
        out_shape=jax.ShapeDtypeStruct((lines, BLK, width), BF16),
        in_specs=[SMEM] + [VMEM] * (1 + len(pieces)),
        out_specs=VMEM,
        scratch_shapes=[
            pltpu.VMEM((nx * ny * 2, BLK, width), BF16),
            pltpu.VMEM((lines, BLK, width), F32),
        ],
        compiler_params=pltpu.CompilerParams(vmem_limit_bytes=VMEM_LIMIT),
    )(table, blocks, *pieces)


def backward_kernel(sizes, table_ref, place_ref, blocks_ref, sibling_ref, own_ref, out_ref, source_ref, total_ref):
    depth, nx, ny = sizes
    source_ref[0 : 2 * depth] = sibling_ref[...]
    source_ref[2 * depth :] = own_ref[...]
    total_ref[...] = jnp.zeros_like(total_ref)
    add_quads(table_ref, 4, 0, table_ref[7, 0], 0, blocks_ref, source_ref, total_ref, 0)
    at_x, at_y = place_ref[2], place_ref[3]
    for oy in range(ny):
        for ox in range(nx):
            y = jnp.bitwise_and(at_y + oy, ny - 1)
            rank = (y // 2 * nx + jnp.bitwise_and(at_x + ox, nx - 1)) * 2 + jnp.bitwise_and(y, 1)
            for h in range(2):
                out_ref[rank, h * BLK : (h + 1) * BLK, :] = total_ref[(oy * nx + ox) * 2 + h].astype(BF16)


def backward_product(table, place, blocks, sibling, own, room, sizes):
    depth, nx, ny = sizes
    lines, _, width = own.shape
    return pl.pallas_call(
        functools.partial(backward_kernel, sizes),
        out_shape=jax.ShapeDtypeStruct((nx * ny, 2 * BLK + room, width), BF16),
        in_specs=[SMEM] * 2 + [VMEM] * 3,
        out_specs=VMEM,
        scratch_shapes=[
            pltpu.VMEM((2 * lines, BLK, width), BF16),
            pltpu.VMEM((nx * ny * 2, BLK, width), F32),
        ],
        cost_estimate=BESIDE,
        compiler_params=pltpu.CompilerParams(vmem_limit_bytes=VMEM_LIMIT),
    )(table, place, blocks, sibling, own)


def hold_kernel(count_ref, blocks_ref, held_ref, mark_ref, sem):
    mark_ref[...] = jnp.zeros_like(mark_ref)
    size = blocks_ref.shape[0] // PARTS
    filled = count_ref[0]

    def part(i):
        at = pl.ds(i * size, size)
        return pltpu.make_async_copy(blocks_ref.at[at], held_ref.at[at], sem.at[i])

    for i in range(PARTS):

        @pl.when(filled > i * size)
        def _(i=i):
            part(i).start()

        @pl.when(filled <= i * size)
        def _(i=i):
            held_ref[pl.ds(i * size, size)] = jnp.zeros((size, *held_ref.shape[1:]), held_ref.dtype)

    for i in range(PARTS):

        @pl.when(filled > i * size)
        def _(i=i):
            part(i).wait()


def hold_blocks(blocks, count):
    return pl.pallas_call(
        hold_kernel,
        out_shape=(pltpu.VMEM(blocks.shape, blocks.dtype), jax.ShapeDtypeStruct((8, BLK), F32)),
        in_specs=[SMEM, pl.BlockSpec(memory_space=pltpu.MemorySpace.HBM)],
        out_specs=(VMEM, VMEM),
        scratch_shapes=[pltpu.SemaphoreType.DMA((PARTS,))],
        compiler_params=pltpu.CompilerParams(vmem_limit_bytes=VMEM_LIMIT),
    )(count, pltpu.with_memory_space_constraint(blocks, pltpu.MemorySpace.HBM))


def dense_kernel(mixed_ref, weight_ref, cotangent_ref, hidden_ref, act_ref, grad_ref):
    weight = weight_ref[...]
    pre_act = jnp.dot(mixed_ref[...], weight, preferred_element_type=F32)
    sigma = jax.nn.sigmoid(pre_act)
    hidden_ref[...] = (pre_act * sigma).astype(BF16)
    slope = sigma * (1.0 + pre_act * (1.0 - sigma))
    act_grad = (cotangent_ref[...].astype(F32) * slope).astype(BF16)
    act_ref[...] = act_grad
    grad_ref[...] = lax.dot_general(
        act_grad, weight, (((1,), (1,)), ((), ())), preferred_element_type=F32
    ).astype(BF16)


def dense(mixed, weight, cotangent):
    shape = jax.ShapeDtypeStruct(cotangent.shape, BF16)
    return pl.pallas_call(
        dense_kernel,
        out_shape=(shape,) * 3,
        compiler_params=pltpu.CompilerParams(vmem_limit_bytes=SMALL_LIMIT),
    )(mixed, weight, cotangent)


def cut(value_ref, at, out_refs):
    size = out_refs[0].shape[0]
    for d, out_ref in enumerate(out_refs):
        owner = jnp.bitwise_and(at + d, len(out_refs) - 1)
        out_ref[...] = value_ref[pl.ds(pl.multiple_of(owner * size, size), size), :]


def weight_shares_kernel(place_ref, mixed_ref, act_ref, *refs):
    *out_refs, value_ref = refs
    value_ref[...] = lax.dot_general(
        mixed_ref[...], act_ref[...], (((0,), (0,)), ((), ())), preferred_element_type=F32
    )
    cut(value_ref, place_ref[2], out_refs)


def weight_shares(place, mixed, act_grad, count):
    rows, width = mixed.shape
    return pl.pallas_call(
        weight_shares_kernel,
        out_shape=(jax.ShapeDtypeStruct((width // count, width), F32),) * count,
        in_specs=[SMEM, VMEM, VMEM],
        out_specs=(VMEM,) * count,
        scratch_shapes=[pltpu.VMEM((width, width), F32)],
        cost_estimate=BESIDE,
        compiler_params=pltpu.CompilerParams(vmem_limit_bytes=SMALL_LIMIT),
    )(place, mixed, act_grad)


def add_cut_kernel(count, place_ref, *refs):
    *refs, value_ref = refs
    terms, out_refs = refs[:4], refs[4:]
    value_ref[...] = (terms[0][...] + terms[1][...]) + (terms[2][...] + terms[3][...])
    if count == 1:
        out_refs[0][...] = value_ref[...]
    else:
        cut(value_ref, place_ref[3], out_refs)


def add_cut(place, terms, count):
    rows, width = terms[0].shape
    return pl.pallas_call(
        functools.partial(add_cut_kernel, count),
        out_shape=(jax.ShapeDtypeStruct((rows // count, width), F32),) * count,
        in_specs=[SMEM] + [VMEM] * 4,
        out_specs=(VMEM,) * count,
        scratch_shapes=[pltpu.VMEM((rows, width), F32)],
        cost_estimate=BESIDE,
        compiler_params=pltpu.CompilerParams(vmem_limit_bytes=SMALL_LIMIT),
    )(place, *terms)


def last_sums_kernel(nx, ny, scale, arrived_ref, feature_ref, weight_ref):
    local = feature_ref.shape[0]
    share = arrived_ref.shape[1] - local
    value = arrived_ref[0, 0:local, :].astype(F32)
    for i in range(1, nx * ny):
        value = value + arrived_ref[i, 0:local, :].astype(F32)
    feature_ref[...] = value.astype(BF16)
    for y in range(ny):
        for x in range(nx):
            rank = (y // 2 * nx + x) * 2 + y % 2
            at = (x * ny + y) * share
            weight_ref[at : at + share, :] = arrived_ref[rank, local:, :].astype(F32) * scale


def last_sums(arrived, local, weight_shape, node_total, sizes):
    _, nx, ny = sizes
    return pl.pallas_call(
        functools.partial(last_sums_kernel, nx, ny, 1.0 / math.sqrt(node_total)),
        out_shape=(
            jax.ShapeDtypeStruct((local, weight_shape[1]), BF16),
            jax.ShapeDtypeStruct(weight_shape, F32),
        ),
        in_specs=[VMEM],
        out_specs=(VMEM,) * 2,
        compiler_params=pltpu.CompilerParams(vmem_limit_bytes=VMEM_LIMIT),
    )(arrived)


def body(sizes, node_features, weight, cotangent, adjacency_blocks, block_coords, block_counts):
    depth, nx, ny = sizes
    together = lax.optimization_barrier
    local, width = node_features.shape
    lanes = width // 2
    node_total = local * nx * ny * depth * 2
    at_x = lax.axis_index("x")
    at_y = lax.axis_index("yh") * 2 + lax.axis_index("yl")
    place = jnp.stack([lax.axis_index("z"), lax.axis_index("c"), at_x, at_y]).astype(jnp.int32)
    count = block_counts.reshape(1)

    def rank(x, y):
        return ((y % ny) // 2 * nx + x % nx) * 2 + y % 2

    def send(value, dx, dy):
        pairs = [(rank(x, y), rank(x + dx, y + dy)) for x in range(nx) for y in range(ny)]
        return lax.ppermute(value, PLANE, pairs)

    def climb(value, dz):
        return lax.ppermute(value, "z", [(i, (i + dz) % depth) for i in range(depth)])

    def swap(value, dz=0, core=True):
        pairs = [(z * 2 + c, (z ^ dz) * 2 + (c ^ int(core))) for z in range(depth) for c in range(2)]
        return lax.ppermute(value, ("z", "c"), pairs)

    with jax.named_scope("gather_features"):
        upright, level = node_features[:, :lanes], node_features[:, lanes:]
        got = together(
            tuple(send(upright, -o, 0) for o in range(1, nx)) + tuple(send(level, 0, -o) for o in range(1, ny))
        )
        upright = jnp.concatenate((upright,) + got[: nx - 1], axis=0)
        level = jnp.concatenate((level,) + got[nx - 1 :], axis=0)
        got = together(
            tuple(send(upright, 0, -o) for o in range(1, ny)) + tuple(send(level, -o, 0) for o in range(1, nx))
        )
        pieces = (upright,) + got[: ny - 1] + (level,) + got[ny - 1 :]

    with jax.named_scope("tables"):
        table = slot_tables(block_coords[0, 0], count, place, sizes)
        table, early = together((table, count))
        blocks, _ = hold_blocks(adjacency_blocks[0, 0], early)

    with jax.named_scope("forward"):
        for_sibling = forward_product(False, table, blocks, pieces, sizes)
        sibling = swap(for_sibling)
        own = forward_product(True, table, blocks, pieces, sizes)
        sibling, own = together((sibling, own))
        own = own.reshape(depth, local, width)
        sibling = sibling.reshape(depth, local, width)

    def term(step):
        return own[step].astype(F32) + sibling[step].astype(F32)

    with jax.named_scope("sum_rows"):
        half = local // 2
        middle = depth // 2
        far = term(middle).astype(BF16)
        up, down = together((climb(far[:half], 1), climb(far[half:], -1)))
        up = jnp.concatenate([up, jnp.zeros_like(up)], axis=0)
        down = jnp.concatenate([jnp.zeros_like(down), down], axis=0)
        for step in range(middle - 1, 0, -1):
            up, down = together(
                ((term(step) + up.astype(F32)).astype(BF16), (term(depth - step) + down.astype(F32)).astype(BF16))
            )
            up, down = together((climb(up, 1), climb(down, -1)))
        mixed = (term(0) + (up.astype(F32) + down.astype(F32))).astype(BF16)

    with jax.named_scope("dense"):
        hidden, act_grad, mixed_grad = dense(mixed, weight, cotangent)

    with jax.named_scope("gather_rows"):

        chunks = {0: mixed_grad}
        ahead = behind = mixed_grad
        for step in range(1, middle + 1):
            if step < middle:
                moved = (climb(ahead, 1), climb(behind, -1))
            else:
                moved = (climb(ahead[:half], 1), climb(behind[half:], -1))
            if step == 1:
                first, *rest = weight_shares(place, mixed, act_grad, nx)
                terms = [first] + [send(value, d + 1, 0) for d, value in enumerate(rest)]
            elif step <= 3:
                terms, _ = together((tuple(terms), ahead))
                first, *rest = add_cut(place, terms, ny if step == 2 else 1)
                if step == 2:
                    terms = [first] + [send(value, 0, d + 1) for d, value in enumerate(rest)]
                else:
                    terms = [first, swap(first, 1, False)]
            else:
                terms, _ = together((tuple(terms), ahead))
                first = terms[0] + terms[1]
                terms = [first, swap(first, 2, False)]
            ahead, behind, terms[0] = together(moved + (terms[0],))
            if step < middle:
                chunks[depth - step] = ahead
                chunks[step] = behind
        chunks[middle] = jnp.concatenate([ahead, behind], axis=0)
        own_panel = jnp.concatenate([chunks[step] for step in range(depth)], axis=0)
        own_panel = own_panel.reshape(2 * depth, BLK, width)
        own_panel, part = together((own_panel, terms[0] + terms[1]))
        sibling_panel = swap(own_panel)
        late, _ = together((count, own_panel))
        part = part + swap(part)
        blocks, mark = hold_blocks(adjacency_blocks[0, 0], late)
        part = part + mark[:1, :1]
        got = swap(part, 4, False)

    with jax.named_scope("backward"):
        share = part.shape[0]
        outs = backward_product(table, place, blocks, sibling_panel, own_panel, share, sizes)
        outs, got, part = together((outs, got, part))
        tail = jnp.broadcast_to((part + got).astype(BF16)[None], (nx * ny, share, width))
        outs = lax.dynamic_update_slice(outs, tail, (0, local, 0))

    with jax.named_scope("sum_columns"):
        arrived = lax.all_to_all(outs, PLANE, 0, 0, tiled=True)
        feature_grad, weight_grad = last_sums(arrived, local, weight.shape, node_total, sizes)
    return (hidden, weight_grad, feature_grad)


def solution(mesh):
    depth = mesh.shape["row"] // 2
    nx = mesh.shape["col"] // 2
    ny = mesh.shape["rep"] * 2
    fine = Mesh(mesh.devices.reshape(depth, 2, ny // 2, nx, 2), ("z", "c", "yh", "x", "yl"))
    row = ("z", "c")
    in_specs = (
        P((*row, *PLANE), None),
        P(),
        P((*PLANE, *row), None),
        P(PLANE, row, None, None, None),
        P(PLANE, row, None, None),
        P(PLANE, row),
    )
    out_specs = (P((*PLANE, *row), None), P(), P((*row, *PLANE), None))
    return jax.shard_map(
        functools.partial(body, (depth, nx, ny)),
        mesh=fine,
        in_specs=in_specs,
        out_specs=out_specs,
        check_vma=False,
    )
```

```python
import functools
import math

import jax
import jax.numpy as jnp
from jax import lax
from jax.experimental import pallas as pl
from jax.experimental.pallas import tpu as pltpu
from jax.sharding import Mesh, PartitionSpec as P

BLK = 128
QUAD = 4
QUADS_A_STEP = 8
PARTS = 8
TABLE = 384
LINES = 32
PLANE = ("yh", "x", "yl")
BF16 = jnp.bfloat16
F32 = jnp.float32
VMEM_LIMIT = 24 * 1024 * 1024
SMALL_LIMIT = 8 * 1024 * 1024
BESIDE = pl.CostEstimate(flops=4_000_000_000, bytes_accessed=0, transcendentals=0)
VMEM = pl.BlockSpec(memory_space=pltpu.VMEM)
SMEM = pl.BlockSpec(memory_space=pltpu.SMEM)


def own_steps(depth):
    middle = depth // 2
    return [(2 * depth, 2)] + [(2 * depth + 2 + 4 * i, 4) for i in range(middle - 1)] + [(4 * depth - 2, 2)]


def slot_tables_kernel(sizes, coords_ref, count_ref, place_ref, table_ref):
    depth, nx, ny = sizes
    slots = coords_ref.shape[1]
    at_z, at_c, at_x, at_y = (place_ref[i] for i in range(4))
    row = coords_ref[0:1, :]
    col = coords_ref[1:2, :]
    away = jnp.bitwise_and((row >> 2) - at_z, depth - 1)
    middle = depth // 2
    spot = jnp.where(away <= middle, 2 * (middle - away) - 1, 2 * (away - middle))
    spot = jnp.where(away == middle, 0, jnp.where(away == 0, depth - 1, spot))
    line_row = jnp.where(jnp.bitwise_and(row >> 1, 1) == at_c, 2 * depth, 0) + spot * 2 + jnp.bitwise_and(row, 1)
    rank = col >> 1
    col_x = jnp.bitwise_and(rank >> 1, nx - 1)
    col_y = rank // (2 * nx) * 2 + jnp.bitwise_and(rank, 1)
    off_x = jnp.bitwise_and(col_x - at_x, nx - 1)
    off_y = jnp.bitwise_and(col_y - at_y, ny - 1)
    line_col = (off_y * nx + off_x) * 2 + jnp.bitwise_and(col, 1)
    lines = jnp.concatenate([line_row, line_col, jnp.zeros((6, slots), jnp.int32)], axis=0).astype(F32)
    columns = jnp.transpose(lines)
    filled = count_ref[0]

    def iota(width, axis):
        return lax.broadcasted_iota(jnp.int32, (slots, width), axis)

    lane, sublane = iota(slots, 1), iota(slots, 0)
    rows = []
    for by in range(2):
        key = jnp.where(iota(1, 0) < filled, columns[:, by : by + 1], 99.0)
        key_lane = jnp.where(lane < filled, jnp.broadcast_to(lines[by : by + 1], (slots, slots)), 99.0)
        key_sub = jnp.broadcast_to(key, (slots, slots))
        ahead = (key_lane == key_sub) & (lane < sublane)
        order = jnp.sum(ahead.astype(F32), axis=1, keepdims=True)
        spot = iota(BLK, 1).astype(F32)
        key_spot = jnp.broadcast_to(key, (slots, BLK))
        held = jnp.sum((key_spot == spot).astype(F32), axis=0, keepdims=True)
        quads = jnp.where(spot[:1] < 99.0, jnp.floor((held + (QUAD - 1)) * (1.0 / QUAD)), 0.0)
        before = jnp.where(spot < key_spot, jnp.broadcast_to(quads, (slots, BLK)), 0.0)
        entry = jnp.sum(before, axis=1, keepdims=True) * QUAD + order
        target = iota(TABLE, 1).astype(F32)
        active = iota(TABLE, 0) < filled
        here = (jnp.broadcast_to(entry, (slots, TABLE)) == target) & active

        def placed(value):
            return jnp.sum(jnp.where(here, jnp.broadcast_to(value, (slots, TABLE)), 0.0), axis=0, keepdims=True)

        spare = (1.0 - placed(jnp.ones((slots, 1), F32))) * LINES
        rows.append(placed(iota(1, 0).astype(F32)))
        rows.append(placed(columns[:, 1 - by : 2 - by]) + spare)
        rows.append(placed(columns[:, by : by + 1]) + spare)
        which = lax.broadcasted_iota(jnp.int32, (1, TABLE), 1)
        marks = jnp.zeros((1, TABLE), F32)
        for i, line in enumerate([LINES] + [begin for begin, _ in own_steps(depth)]):
            ahead = jnp.sum(jnp.where(spot[:1] < line, quads, 0.0), axis=1, keepdims=True)
            marks = jnp.where(which == i, jnp.broadcast_to(ahead, (1, TABLE)), marks)
        rows.append(marks)
    table_ref[...] = jnp.concatenate(rows, axis=0).astype(jnp.int32)


def slot_tables(coords, count, place, sizes):
    return pl.pallas_call(
        functools.partial(slot_tables_kernel, sizes),
        out_shape=jax.ShapeDtypeStruct((8, TABLE), jnp.int32),
        in_specs=[VMEM, SMEM, SMEM],
        out_specs=VMEM,
        compiler_params=pltpu.CompilerParams(vmem_limit_bytes=SMALL_LIMIT),
    )(coords, count, place)


def add_quads(table_ref, base, begin, end, first_line, blocks_ref, source_ref, total_ref, contract):
    def quad(at):
        entries = [at * QUAD + u for u in range(QUAD)]
        lefts = [blocks_ref[table_ref[base, e]] for e in entries]
        rights = [source_ref[table_ref[base + 1, e]] for e in entries]
        product = None
        for u in range(0, QUAD, 2):
            left = jnp.concatenate(lefts[u : u + 2], axis=contract)
            right = jnp.concatenate(rights[u : u + 2], axis=0)
            term = lax.dot_general(left, right, (((contract,), (0,)), ((), ())), preferred_element_type=F32)
            product = term if product is None else product + term
        return table_ref[base + 2, entries[0]] - first_line, product

    @pl.loop(0, (end - begin + QUADS_A_STEP - 1) // QUADS_A_STEP)
    def _(i):
        found = [quad(begin + i * QUADS_A_STEP + j) for j in range(QUADS_A_STEP)]
        for line, product in found:
            total_ref[line] += product


def sibling_rows_kernel(sizes, table_ref, blocks_ref, *refs):
    depth, nx, ny = sizes
    *piece_refs, out_ref, source_ref, total_ref = refs
    lanes = piece_refs[0].shape[-1]
    for oy in range(ny):
        for ox in range(nx):
            for h in range(2):
                for half, major, minor in ((0, oy, ox), (1, ox, oy)):
                    piece = piece_refs[half * ny + major]
                    source_ref[(oy * nx + ox) * 2 + h, :, half * lanes : (half + 1) * lanes] = piece[
                        pl.ds((minor * 2 + h) * BLK, BLK), :
                    ]
    source_ref[LINES] = jnp.zeros_like(source_ref[LINES])
    count = out_ref.shape[0]
    total_ref[0:count] = jnp.zeros(out_ref.shape, F32)
    add_quads(table_ref, 0, 0, table_ref[3, 1], 0, blocks_ref, source_ref, total_ref, 1)
    out_ref[...] = total_ref[0:count].astype(BF16)


def sibling_rows(table, blocks, pieces, sizes):
    width = 2 * pieces[0].shape[-1]
    return pl.pallas_call(
        functools.partial(sibling_rows_kernel, sizes),
        out_shape=(
            jax.ShapeDtypeStruct((2 * sizes[0], BLK, width), BF16),
            jax.ShapeDtypeStruct((LINES + 1, BLK, width), BF16),
        ),
        in_specs=[SMEM] + [VMEM] * (1 + len(pieces)),
        out_specs=(VMEM, VMEM),
        scratch_shapes=[pltpu.VMEM((LINES + 1, BLK, width), F32)],
        compiler_params=pltpu.CompilerParams(vmem_limit_bytes=VMEM_LIMIT),
    )(table, blocks, *pieces)


def own_rows_kernel(step, depth, table_ref, blocks_ref, source_ref, out_ref, total_ref):
    steps = own_steps(depth)
    first, count = steps[step]
    total_ref[0:count] = jnp.zeros(out_ref.shape, F32)
    begin = table_ref[3, 1 + step]
    end = table_ref[3, 2 + step] if step + 1 < len(steps) else table_ref[3, 0]
    add_quads(table_ref, 0, begin, end, first, blocks_ref, source_ref, total_ref, 1)
    out_ref[...] = total_ref[0:count].astype(BF16)


def own_rows(step, table, blocks, source, depth):
    first, count = own_steps(depth)[step]
    width = source.shape[2]
    return pl.pallas_call(
        functools.partial(own_rows_kernel, step, depth),
        out_shape=jax.ShapeDtypeStruct((count, BLK, width), BF16),
        in_specs=[SMEM, VMEM, VMEM],
        out_specs=VMEM,
        scratch_shapes=[pltpu.VMEM((LINES + 1 - first, BLK, width), F32)],
        cost_estimate=BESIDE,
        compiler_params=pltpu.CompilerParams(vmem_limit_bytes=VMEM_LIMIT),
    )(table, blocks, source)


def backward_kernel(sizes, table_ref, place_ref, blocks_ref, sibling_ref, own_ref, out_ref, source_ref, total_ref):
    depth, nx, ny = sizes
    source_ref[0 : 2 * depth] = sibling_ref[...]
    source_ref[2 * depth : LINES] = own_ref[...]
    source_ref[LINES] = jnp.zeros_like(source_ref[LINES])
    total_ref[0:LINES] = jnp.zeros((LINES, *total_ref.shape[1:]), F32)
    add_quads(table_ref, 4, 0, table_ref[7, 0], 0, blocks_ref, source_ref, total_ref, 0)
    at_x, at_y = place_ref[2], place_ref[3]
    for oy in range(ny):
        for ox in range(nx):
            y = jnp.bitwise_and(at_y + oy, ny - 1)
            rank = (y // 2 * nx + jnp.bitwise_and(at_x + ox, nx - 1)) * 2 + jnp.bitwise_and(y, 1)
            for h in range(2):
                out_ref[rank, h * BLK : (h + 1) * BLK, :] = total_ref[(oy * nx + ox) * 2 + h].astype(BF16)


def backward_product(table, place, blocks, sibling, own, room, sizes):
    depth, nx, ny = sizes
    lines, _, width = own.shape
    return pl.pallas_call(
        functools.partial(backward_kernel, sizes),
        out_shape=jax.ShapeDtypeStruct((nx * ny, 2 * BLK + room, width), BF16),
        in_specs=[SMEM] * 2 + [VMEM] * 3,
        out_specs=VMEM,
        scratch_shapes=[
            pltpu.VMEM((LINES + 1, BLK, width), BF16),
            pltpu.VMEM((LINES + 1, BLK, width), F32),
        ],
        cost_estimate=BESIDE,
        compiler_params=pltpu.CompilerParams(vmem_limit_bytes=VMEM_LIMIT),
    )(table, place, blocks, sibling, own)


def hold_kernel(count_ref, blocks_ref, held_ref, mark_ref, sem):
    mark_ref[...] = jnp.zeros_like(mark_ref)
    size = blocks_ref.shape[0] // PARTS
    filled = count_ref[0]

    def part(i):
        at = pl.ds(i * size, size)
        return pltpu.make_async_copy(blocks_ref.at[at], held_ref.at[at], sem.at[i])

    for i in range(PARTS):

        @pl.when(filled > i * size)
        def _(i=i):
            part(i).start()

        @pl.when(filled <= i * size)
        def _(i=i):
            held_ref[pl.ds(i * size, size)] = jnp.zeros((size, *held_ref.shape[1:]), held_ref.dtype)

    for i in range(PARTS):

        @pl.when(filled > i * size)
        def _(i=i):
            part(i).wait()


def hold_blocks(blocks, count):
    return pl.pallas_call(
        hold_kernel,
        out_shape=(pltpu.VMEM(blocks.shape, blocks.dtype), jax.ShapeDtypeStruct((8, BLK), F32)),
        in_specs=[SMEM, pl.BlockSpec(memory_space=pltpu.MemorySpace.HBM)],
        out_specs=(VMEM, VMEM),
        scratch_shapes=[pltpu.SemaphoreType.DMA((PARTS,))],
        compiler_params=pltpu.CompilerParams(vmem_limit_bytes=VMEM_LIMIT),
    )(count, pltpu.with_memory_space_constraint(blocks, pltpu.MemorySpace.HBM))


def panel_kernel(*refs):
    *chunk_refs, panel_ref = refs
    at = 0
    for ref in chunk_refs:
        for begin in range(0, ref.shape[0], BLK):
            panel_ref[at] = ref[begin : begin + BLK, :]
            at += 1


def own_rows_panel(chunks):
    width = chunks[0].shape[1]
    lines = sum(chunk.shape[0] for chunk in chunks) // BLK
    return pl.pallas_call(
        panel_kernel,
        out_shape=jax.ShapeDtypeStruct((lines, BLK, width), BF16),
        in_specs=[VMEM] * len(chunks),
        out_specs=VMEM,
        compiler_params=pltpu.CompilerParams(vmem_limit_bytes=SMALL_LIMIT),
    )(*chunks)


def dense_kernel(mixed_ref, weight_ref, cotangent_ref, hidden_ref, act_ref, grad_ref):
    weight = weight_ref[...]
    pre_act = jnp.dot(mixed_ref[...], weight, preferred_element_type=F32)
    sigma = jax.nn.sigmoid(pre_act)
    hidden_ref[...] = (pre_act * sigma).astype(BF16)
    slope = sigma * (1.0 + pre_act * (1.0 - sigma))
    act_grad = (cotangent_ref[...].astype(F32) * slope).astype(BF16)
    act_ref[...] = act_grad
    grad_ref[...] = lax.dot_general(
        act_grad, weight, (((1,), (1,)), ((), ())), preferred_element_type=F32
    ).astype(BF16)


def dense(mixed, weight, cotangent):
    shape = jax.ShapeDtypeStruct(cotangent.shape, BF16)
    return pl.pallas_call(
        dense_kernel,
        out_shape=(shape,) * 3,
        compiler_params=pltpu.CompilerParams(vmem_limit_bytes=SMALL_LIMIT),
    )(mixed, weight, cotangent)


def cut(value_ref, at, out_refs):
    size = out_refs[0].shape[0]
    for d, out_ref in enumerate(out_refs):
        owner = jnp.bitwise_and(at + d, len(out_refs) - 1)
        out_ref[...] = value_ref[pl.ds(pl.multiple_of(owner * size, size), size), :]


def weight_shares_kernel(place_ref, mixed_ref, act_ref, *refs):
    *out_refs, value_ref = refs
    value_ref[...] = lax.dot_general(
        mixed_ref[...], act_ref[...], (((0,), (0,)), ((), ())), preferred_element_type=F32
    )
    cut(value_ref, place_ref[2], out_refs)


def weight_shares(place, mixed, act_grad, count):
    rows, width = mixed.shape
    return pl.pallas_call(
        weight_shares_kernel,
        out_shape=(jax.ShapeDtypeStruct((width // count, width), F32),) * count,
        in_specs=[SMEM, VMEM, VMEM],
        out_specs=(VMEM,) * count,
        scratch_shapes=[pltpu.VMEM((width, width), F32)],
        cost_estimate=BESIDE,
        compiler_params=pltpu.CompilerParams(vmem_limit_bytes=SMALL_LIMIT),
    )(place, mixed, act_grad)


def add_cut_kernel(count, place_ref, *refs):
    *refs, value_ref = refs
    terms, out_refs = refs[:4], refs[4:]
    value_ref[...] = (terms[0][...] + terms[1][...]) + (terms[2][...] + terms[3][...])
    if count == 1:
        out_refs[0][...] = value_ref[...]
    else:
        cut(value_ref, place_ref[3], out_refs)


def add_cut(place, terms, count):
    rows, width = terms[0].shape
    return pl.pallas_call(
        functools.partial(add_cut_kernel, count),
        out_shape=(jax.ShapeDtypeStruct((rows // count, width), F32),) * count,
        in_specs=[SMEM] + [VMEM] * 4,
        out_specs=(VMEM,) * count,
        scratch_shapes=[pltpu.VMEM((rows, width), F32)],
        cost_estimate=BESIDE,
        compiler_params=pltpu.CompilerParams(vmem_limit_bytes=SMALL_LIMIT),
    )(place, *terms)


def last_sums_kernel(nx, ny, scale, arrived_ref, feature_ref, weight_ref):
    local = feature_ref.shape[0]
    share = arrived_ref.shape[1] - local
    value = arrived_ref[0, 0:local, :].astype(F32)
    for i in range(1, nx * ny):
        value = value + arrived_ref[i, 0:local, :].astype(F32)
    feature_ref[...] = value.astype(BF16)
    for y in range(ny):
        for x in range(nx):
            rank = (y // 2 * nx + x) * 2 + y % 2
            at = (x * ny + y) * share
            weight_ref[at : at + share, :] = arrived_ref[rank, local:, :].astype(F32) * scale


def last_sums(arrived, local, weight_shape, node_total, sizes):
    _, nx, ny = sizes
    return pl.pallas_call(
        functools.partial(last_sums_kernel, nx, ny, 1.0 / math.sqrt(node_total)),
        out_shape=(
            jax.ShapeDtypeStruct((local, weight_shape[1]), BF16),
            jax.ShapeDtypeStruct(weight_shape, F32),
        ),
        in_specs=[VMEM],
        out_specs=(VMEM,) * 2,
        compiler_params=pltpu.CompilerParams(vmem_limit_bytes=VMEM_LIMIT),
    )(arrived)


def body(sizes, node_features, weight, cotangent, adjacency_blocks, block_coords, block_counts):
    depth, nx, ny = sizes
    together = lax.optimization_barrier
    local, width = node_features.shape
    lanes = width // 2
    node_total = local * nx * ny * depth * 2
    at_x = lax.axis_index("x")
    at_y = lax.axis_index("yh") * 2 + lax.axis_index("yl")
    place = jnp.stack([lax.axis_index("z"), lax.axis_index("c"), at_x, at_y]).astype(jnp.int32)
    count = block_counts.reshape(1)

    def rank(x, y):
        return ((y % ny) // 2 * nx + x % nx) * 2 + y % 2

    def send(value, dx, dy):
        pairs = [(rank(x, y), rank(x + dx, y + dy)) for x in range(nx) for y in range(ny)]
        return lax.ppermute(value, PLANE, pairs)

    def climb(value, dz):
        return lax.ppermute(value, "z", [(i, (i + dz) % depth) for i in range(depth)])

    def swap(value, dz=0, core=True):
        pairs = [(z * 2 + c, (z ^ dz) * 2 + (c ^ int(core))) for z in range(depth) for c in range(2)]
        return lax.ppermute(value, ("z", "c"), pairs)

    with jax.named_scope("gather_features"):
        upright, level = node_features[:, :lanes], node_features[:, lanes:]
        shifts = [1, nx - 1] + list(range(2, nx - 1))

        def halves(across, along):
            got = [(send(across, -o, 0), send(along, 0, -o)) for o in shifts]
            got = together(tuple(value for pair in got for value in pair))
            first, second = dict(zip(shifts, got[0::2])), dict(zip(shifts, got[1::2]))
            return [first[o] for o in range(1, nx)], [second[o] for o in range(1, ny)]

        at_side, at_line = halves(upright, level)
        upright = jnp.concatenate([upright] + at_side, axis=0)
        level = jnp.concatenate([level] + at_line, axis=0)
        at_side, at_line = halves(level, upright)
        pieces = (upright, *at_line, level, *at_side)

    with jax.named_scope("tables"):
        table = slot_tables(block_coords[0, 0], count, place, sizes)
        table, early = together((table, count))
        blocks, _ = hold_blocks(adjacency_blocks[0, 0], early)

    with jax.named_scope("forward"):
        for_sibling, source = sibling_rows(table, blocks, pieces, sizes)
        sibling = swap(for_sibling)
        own = own_rows(0, table, blocks, source, depth)
        sibling, own = together((sibling, own))
        sibling = sibling.reshape(depth, local, width)

    def term(mine, spot):
        return mine.astype(F32) + sibling[spot].astype(F32)

    with jax.named_scope("sum_rows"):
        half = local // 2
        middle = depth // 2
        far = term(own.reshape(local, width), 0).astype(BF16)
        up, down = far[:half], far[half:]
        for step in range(1, middle + 1):
            pace, up, down = together((table, up, down))
            own = own_rows(step, pace, blocks, source, depth)
            up, down = together((climb(up, 1), climb(down, -1)))
            if step == 1:
                up = jnp.concatenate([up, jnp.zeros_like(up)], axis=0)
                down = jnp.concatenate([jnp.zeros_like(down), down], axis=0)
            mine = own.reshape(-1, local, width)
            if step < middle:
                up = (term(mine[0], 2 * step - 1) + up.astype(F32)).astype(BF16)
                down = (term(mine[1], 2 * step) + down.astype(F32)).astype(BF16)
            else:
                mixed = (term(mine[0], depth - 1) + (up.astype(F32) + down.astype(F32))).astype(BF16)

    with jax.named_scope("dense"):
        hidden, act_grad, mixed_grad = dense(mixed, weight, cotangent)

    with jax.named_scope("gather_rows"):

        chunks = {0: mixed_grad}
        ahead = behind = mixed_grad
        for step in range(1, middle + 1):
            if step < middle:
                moved = (climb(ahead, 1), climb(behind, -1))
            else:
                moved = (climb(ahead[:half], 1), climb(behind[half:], -1))
            if step == 1:
                first, *rest = weight_shares(place, mixed, act_grad, nx)
                terms = [first] + [send(value, d + 1, 0) for d, value in enumerate(rest)]
            elif step <= 3:
                terms, _ = together((tuple(terms), ahead))
                first, *rest = add_cut(place, terms, ny if step == 2 else 1)
                if step == 2:
                    terms = [first] + [send(value, 0, d + 1) for d, value in enumerate(rest)]
                else:
                    terms = [first, swap(first, 1, False)]
            else:
                terms, _ = together((tuple(terms), ahead))
                first = terms[0] + terms[1]
                terms = [first, swap(first, 2, False)]
            ahead, behind, terms[0] = together(moved + (terms[0],))
            if step > 2:
                ahead, behind, *terms = together((ahead, behind, *terms))
            if step < middle:
                chunks[depth - step] = ahead
                chunks[step] = behind
        order = [d for i in range(1, middle) for d in (middle - i, middle + i)] + [0]
        own_panel = own_rows_panel([ahead, behind] + [chunks[d] for d in order])
        own_panel, part = together((own_panel, terms[0] + terms[1]))
        sibling_panel = swap(own_panel)
        part = part + swap(part)
        got = swap(part, 4, False)

    with jax.named_scope("backward"):
        share = part.shape[0]
        outs = backward_product(table, place, blocks, sibling_panel, own_panel, share, sizes)
        outs, got, part = together((outs, got, part))
        tail = jnp.broadcast_to((part + got).astype(BF16)[None], (nx * ny, share, width))
        outs = lax.dynamic_update_slice(outs, tail, (0, local, 0))

    with jax.named_scope("sum_columns"):
        arrived = lax.all_to_all(outs, PLANE, 0, 0, tiled=True)
        feature_grad, weight_grad = last_sums(arrived, local, weight.shape, node_total, sizes)
    return (hidden, weight_grad, feature_grad)


def solution(mesh):
    depth = mesh.shape["row"] // 2
    nx = mesh.shape["col"] // 2
    ny = mesh.shape["rep"] * 2
    fine = Mesh(mesh.devices.reshape(depth, 2, ny // 2, nx, 2), ("z", "c", "yh", "x", "yl"))
    row = ("z", "c")
    in_specs = (
        P((*row, *PLANE), None),
        P(),
        P((*PLANE, *row), None),
        P(PLANE, row, None, None, None),
        P(PLANE, row, None, None),
        P(PLANE, row),
    )
    out_specs = (P((*PLANE, *row), None), P(), P((*row, *PLANE), None))
    return jax.shard_map(
        functools.partial(body, (depth, nx, ny)),
        mesh=fine,
        in_specs=in_specs,
        out_specs=out_specs,
        check_vma=False,
    )
```

```python
import functools
import math

import jax
import jax.numpy as jnp
from jax import lax
from jax.experimental import pallas as pl
from jax.experimental.pallas import tpu as pltpu
from jax.sharding import Mesh, PartitionSpec as P

BLK = 128
QUAD = 4
QUADS_A_STEP = 8
PARTS = 8
TABLE = 384
LINES = 32
PLANE = ("yh", "x", "yl")
BF16 = jnp.bfloat16
F32 = jnp.float32
VMEM_LIMIT = 24 * 1024 * 1024
SMALL_LIMIT = 8 * 1024 * 1024
BESIDE = pl.CostEstimate(flops=4_000_000_000, bytes_accessed=0, transcendentals=0)
VMEM = pl.BlockSpec(memory_space=pltpu.VMEM)
SMEM = pl.BlockSpec(memory_space=pltpu.SMEM)


def own_steps(depth):
    return [(2 * depth + 4 * i, 4) for i in range(depth // 2)]


def slot_tables_kernel(sizes, coords_ref, count_ref, place_ref, table_ref):
    depth, nx, ny = sizes
    slots = coords_ref.shape[1]
    at_z, at_c, at_x, at_y = (place_ref[i] for i in range(4))
    row = coords_ref[0:1, :]
    col = coords_ref[1:2, :]
    away = jnp.bitwise_and((row >> 2) - at_z, depth - 1)
    middle = depth // 2
    spot = jnp.where(away < middle, 2 * (middle - away), 2 * (away - middle) + 1)
    spot = jnp.where(away == middle, 0, jnp.where(away == 0, 1, spot))
    line_row = jnp.where(jnp.bitwise_and(row >> 1, 1) == at_c, 2 * depth, 0) + spot * 2 + jnp.bitwise_and(row, 1)
    rank = col >> 1
    col_x = jnp.bitwise_and(rank >> 1, nx - 1)
    col_y = rank // (2 * nx) * 2 + jnp.bitwise_and(rank, 1)
    off_x = jnp.bitwise_and(col_x - at_x, nx - 1)
    off_y = jnp.bitwise_and(col_y - at_y, ny - 1)
    line_col = (off_y * nx + off_x) * 2 + jnp.bitwise_and(col, 1)
    lines = jnp.concatenate([line_row, line_col, jnp.zeros((6, slots), jnp.int32)], axis=0).astype(F32)
    columns = jnp.transpose(lines)
    filled = count_ref[0]

    def iota(width, axis):
        return lax.broadcasted_iota(jnp.int32, (slots, width), axis)

    lane, sublane = iota(slots, 1), iota(slots, 0)
    rows = []
    for by in range(2):
        key = jnp.where(iota(1, 0) < filled, columns[:, by : by + 1], 99.0)
        key_lane = jnp.where(lane < filled, jnp.broadcast_to(lines[by : by + 1], (slots, slots)), 99.0)
        key_sub = jnp.broadcast_to(key, (slots, slots))
        ahead = (key_lane == key_sub) & (lane < sublane)
        order = jnp.sum(ahead.astype(F32), axis=1, keepdims=True)
        spot = iota(BLK, 1).astype(F32)
        key_spot = jnp.broadcast_to(key, (slots, BLK))
        held = jnp.sum((key_spot == spot).astype(F32), axis=0, keepdims=True)
        quads = jnp.where(spot[:1] < 99.0, jnp.floor((held + (QUAD - 1)) * (1.0 / QUAD)), 0.0)
        before = jnp.where(spot < key_spot, jnp.broadcast_to(quads, (slots, BLK)), 0.0)
        entry = jnp.sum(before, axis=1, keepdims=True) * QUAD + order
        target = iota(TABLE, 1).astype(F32)
        active = iota(TABLE, 0) < filled
        here = (jnp.broadcast_to(entry, (slots, TABLE)) == target) & active

        def placed(value):
            return jnp.sum(jnp.where(here, jnp.broadcast_to(value, (slots, TABLE)), 0.0), axis=0, keepdims=True)

        spare = (1.0 - placed(jnp.ones((slots, 1), F32))) * LINES
        rows.append(placed(iota(1, 0).astype(F32)))
        rows.append(placed(columns[:, 1 - by : 2 - by]) + spare)
        rows.append(placed(columns[:, by : by + 1]) + spare)
        which = lax.broadcasted_iota(jnp.int32, (1, TABLE), 1)
        marks = jnp.zeros((1, TABLE), F32)
        for i, line in enumerate([LINES] + [begin for begin, _ in own_steps(depth)]):
            ahead = jnp.sum(jnp.where(spot[:1] < line, quads, 0.0), axis=1, keepdims=True)
            marks = jnp.where(which == i, jnp.broadcast_to(ahead, (1, TABLE)), marks)
        rows.append(marks)
    table_ref[...] = jnp.concatenate(rows, axis=0).astype(jnp.int32)


def slot_tables(coords, count, place, sizes):
    return pl.pallas_call(
        functools.partial(slot_tables_kernel, sizes),
        out_shape=jax.ShapeDtypeStruct((8, TABLE), jnp.int32),
        in_specs=[VMEM, SMEM, SMEM],
        out_specs=VMEM,
        compiler_params=pltpu.CompilerParams(vmem_limit_bytes=SMALL_LIMIT),
    )(coords, count, place)


def add_quads(table_ref, base, begin, end, first_line, blocks_ref, source_ref, total_ref, contract):
    def quad(at):
        entries = [at * QUAD + u for u in range(QUAD)]
        lefts = [blocks_ref[table_ref[base, e]] for e in entries]
        rights = [source_ref[table_ref[base + 1, e]] for e in entries]
        product = None
        for u in range(0, QUAD, 2):
            left = jnp.concatenate(lefts[u : u + 2], axis=contract)
            right = jnp.concatenate(rights[u : u + 2], axis=0)
            term = lax.dot_general(left, right, (((contract,), (0,)), ((), ())), preferred_element_type=F32)
            product = term if product is None else product + term
        return table_ref[base + 2, entries[0]] - first_line, product

    @pl.loop(0, (end - begin + QUADS_A_STEP - 1) // QUADS_A_STEP)
    def _(i):
        found = [quad(begin + i * QUADS_A_STEP + j) for j in range(QUADS_A_STEP)]
        for line, product in found:
            total_ref[line] += product


def sibling_rows_kernel(sizes, table_ref, blocks_ref, *refs):
    depth, nx, ny = sizes
    *piece_refs, out_ref, source_ref, total_ref = refs
    lanes = piece_refs[0].shape[-1]
    for oy in range(ny):
        for ox in range(nx):
            for h in range(2):
                for half, major, minor in ((0, oy, ox), (1, ox, oy)):
                    piece = piece_refs[half * ny + major]
                    source_ref[(oy * nx + ox) * 2 + h, :, half * lanes : (half + 1) * lanes] = piece[
                        pl.ds((minor * 2 + h) * BLK, BLK), :
                    ]
    source_ref[LINES] = jnp.zeros_like(source_ref[LINES])
    count = out_ref.shape[0]
    total_ref[0:count] = jnp.zeros(out_ref.shape, F32)
    add_quads(table_ref, 0, 0, table_ref[3, 1], 0, blocks_ref, source_ref, total_ref, 1)
    out_ref[...] = total_ref[0:count].astype(BF16)


def sibling_rows(table, blocks, pieces, sizes):
    width = 2 * pieces[0].shape[-1]
    return pl.pallas_call(
        functools.partial(sibling_rows_kernel, sizes),
        out_shape=(
            jax.ShapeDtypeStruct((2 * sizes[0], BLK, width), BF16),
            jax.ShapeDtypeStruct((LINES + 1, BLK, width), BF16),
        ),
        in_specs=[SMEM] + [VMEM] * (1 + len(pieces)),
        out_specs=(VMEM, VMEM),
        scratch_shapes=[pltpu.VMEM((LINES + 1, BLK, width), F32)],
        compiler_params=pltpu.CompilerParams(vmem_limit_bytes=VMEM_LIMIT),
    )(table, blocks, *pieces)


def own_rows_kernel(step, depth, table_ref, blocks_ref, source_ref, out_ref, total_ref):
    steps = own_steps(depth)
    first, count = steps[step]
    total_ref[0:count] = jnp.zeros(out_ref.shape, F32)
    begin = table_ref[3, 1 + step]
    end = table_ref[3, 2 + step] if step + 1 < len(steps) else table_ref[3, 0]
    add_quads(table_ref, 0, begin, end, first, blocks_ref, source_ref, total_ref, 1)
    out_ref[...] = total_ref[0:count].astype(BF16)


def own_rows(step, table, blocks, source, depth):
    first, count = own_steps(depth)[step]
    width = source.shape[2]
    return pl.pallas_call(
        functools.partial(own_rows_kernel, step, depth),
        out_shape=jax.ShapeDtypeStruct((count, BLK, width), BF16),
        in_specs=[SMEM, VMEM, VMEM],
        out_specs=VMEM,
        scratch_shapes=[pltpu.VMEM((LINES + 1 - first, BLK, width), F32)],
        cost_estimate=BESIDE,
        compiler_params=pltpu.CompilerParams(vmem_limit_bytes=VMEM_LIMIT),
    )(table, blocks, source)


def backward_kernel(sizes, table_ref, place_ref, blocks_ref, sibling_ref, own_ref, out_ref, source_ref, total_ref):
    depth, nx, ny = sizes
    source_ref[0 : 2 * depth] = sibling_ref[...]
    source_ref[2 * depth : LINES] = own_ref[...]
    source_ref[LINES] = jnp.zeros_like(source_ref[LINES])
    total_ref[0:LINES] = jnp.zeros((LINES, *total_ref.shape[1:]), F32)
    add_quads(table_ref, 4, 0, table_ref[7, 0], 0, blocks_ref, source_ref, total_ref, 0)
    at_x, at_y = place_ref[2], place_ref[3]
    for oy in range(ny):
        for ox in range(nx):
            y = jnp.bitwise_and(at_y + oy, ny - 1)
            rank = (y // 2 * nx + jnp.bitwise_and(at_x + ox, nx - 1)) * 2 + jnp.bitwise_and(y, 1)
            for h in range(2):
                out_ref[rank, h * BLK : (h + 1) * BLK, :] = total_ref[(oy * nx + ox) * 2 + h].astype(BF16)


def backward_product(table, place, blocks, sibling, own, room, sizes):
    depth, nx, ny = sizes
    lines, _, width = own.shape
    return pl.pallas_call(
        functools.partial(backward_kernel, sizes),
        out_shape=jax.ShapeDtypeStruct((nx * ny, 2 * BLK + room, width), BF16),
        in_specs=[SMEM] * 2 + [VMEM] * 3,
        out_specs=VMEM,
        scratch_shapes=[
            pltpu.VMEM((LINES + 1, BLK, width), BF16),
            pltpu.VMEM((LINES + 1, BLK, width), F32),
        ],
        cost_estimate=BESIDE,
        compiler_params=pltpu.CompilerParams(vmem_limit_bytes=VMEM_LIMIT),
    )(table, place, blocks, sibling, own)


def hold_kernel(count_ref, blocks_ref, held_ref, mark_ref, sem):
    mark_ref[...] = jnp.zeros_like(mark_ref)
    size = blocks_ref.shape[0] // PARTS
    filled = count_ref[0]

    def part(i):
        at = pl.ds(i * size, size)
        return pltpu.make_async_copy(blocks_ref.at[at], held_ref.at[at], sem.at[i])

    for i in range(PARTS):

        @pl.when(filled > i * size)
        def _(i=i):
            part(i).start()

        @pl.when(filled <= i * size)
        def _(i=i):
            held_ref[pl.ds(i * size, size)] = jnp.zeros((size, *held_ref.shape[1:]), held_ref.dtype)

    for i in range(PARTS):

        @pl.when(filled > i * size)
        def _(i=i):
            part(i).wait()


def hold_blocks(blocks, count):
    return pl.pallas_call(
        hold_kernel,
        out_shape=(pltpu.VMEM(blocks.shape, blocks.dtype), jax.ShapeDtypeStruct((8, BLK), F32)),
        in_specs=[SMEM, pl.BlockSpec(memory_space=pltpu.MemorySpace.HBM)],
        out_specs=(VMEM, VMEM),
        scratch_shapes=[pltpu.SemaphoreType.DMA((PARTS,))],
        compiler_params=pltpu.CompilerParams(vmem_limit_bytes=VMEM_LIMIT),
    )(count, pltpu.with_memory_space_constraint(blocks, pltpu.MemorySpace.HBM))


def panel_kernel(*refs):
    *chunk_refs, panel_ref = refs
    at = 0
    for ref in chunk_refs:
        for begin in range(0, ref.shape[0], BLK):
            panel_ref[at] = ref[begin : begin + BLK, :]
            at += 1


def own_rows_panel(chunks):
    width = chunks[0].shape[1]
    lines = sum(chunk.shape[0] for chunk in chunks) // BLK
    return pl.pallas_call(
        panel_kernel,
        out_shape=jax.ShapeDtypeStruct((lines, BLK, width), BF16),
        in_specs=[VMEM] * len(chunks),
        out_specs=VMEM,
        compiler_params=pltpu.CompilerParams(vmem_limit_bytes=SMALL_LIMIT),
    )(*chunks)


def dense_kernel(mixed_ref, weight_ref, cotangent_ref, hidden_ref, act_ref, grad_ref):
    weight = weight_ref[...]
    pre_act = jnp.dot(mixed_ref[...], weight, preferred_element_type=F32)
    sigma = jax.nn.sigmoid(pre_act)
    hidden_ref[...] = (pre_act * sigma).astype(BF16)
    slope = sigma * (1.0 + pre_act * (1.0 - sigma))
    act_grad = (cotangent_ref[...].astype(F32) * slope).astype(BF16)
    act_ref[...] = act_grad
    grad_ref[...] = lax.dot_general(
        act_grad, weight, (((1,), (1,)), ((), ())), preferred_element_type=F32
    ).astype(BF16)


def dense(mixed, weight, cotangent):
    shape = jax.ShapeDtypeStruct(cotangent.shape, BF16)
    return pl.pallas_call(
        dense_kernel,
        out_shape=(shape,) * 3,
        compiler_params=pltpu.CompilerParams(vmem_limit_bytes=SMALL_LIMIT),
    )(mixed, weight, cotangent)


def cut(value_ref, at, out_refs):
    size = out_refs[0].shape[0]
    for d, out_ref in enumerate(out_refs):
        owner = jnp.bitwise_and(at + d, len(out_refs) - 1)
        out_ref[...] = value_ref[pl.ds(pl.multiple_of(owner * size, size), size), :]


def weight_shares_kernel(place_ref, mixed_ref, act_ref, *refs):
    *out_refs, value_ref = refs
    value_ref[...] = lax.dot_general(
        mixed_ref[...], act_ref[...], (((0,), (0,)), ((), ())), preferred_element_type=F32
    )
    cut(value_ref, place_ref[2], out_refs)


def weight_shares(place, mixed, act_grad, count):
    rows, width = mixed.shape
    return pl.pallas_call(
        weight_shares_kernel,
        out_shape=(jax.ShapeDtypeStruct((width // count, width), F32),) * count,
        in_specs=[SMEM, VMEM, VMEM],
        out_specs=(VMEM,) * count,
        scratch_shapes=[pltpu.VMEM((width, width), F32)],
        cost_estimate=BESIDE,
        compiler_params=pltpu.CompilerParams(vmem_limit_bytes=SMALL_LIMIT),
    )(place, mixed, act_grad)


def add_cut_kernel(count, place_ref, *refs):
    *refs, value_ref = refs
    terms, out_refs = refs[:4], refs[4:]
    value_ref[...] = (terms[0][...] + terms[1][...]) + (terms[2][...] + terms[3][...])
    if count == 1:
        out_refs[0][...] = value_ref[...]
    else:
        cut(value_ref, place_ref[3], out_refs)


def add_cut(place, terms, count):
    rows, width = terms[0].shape
    return pl.pallas_call(
        functools.partial(add_cut_kernel, count),
        out_shape=(jax.ShapeDtypeStruct((rows // count, width), F32),) * count,
        in_specs=[SMEM] + [VMEM] * 4,
        out_specs=(VMEM,) * count,
        scratch_shapes=[pltpu.VMEM((rows, width), F32)],
        cost_estimate=BESIDE,
        compiler_params=pltpu.CompilerParams(vmem_limit_bytes=SMALL_LIMIT),
    )(place, *terms)


def last_sums_kernel(nx, ny, scale, arrived_ref, feature_ref, weight_ref):
    local = feature_ref.shape[0]
    share = arrived_ref.shape[1] - local
    value = arrived_ref[0, 0:local, :].astype(F32)
    for i in range(1, nx * ny):
        value = value + arrived_ref[i, 0:local, :].astype(F32)
    feature_ref[...] = value.astype(BF16)
    for y in range(ny):
        for x in range(nx):
            rank = (y // 2 * nx + x) * 2 + y % 2
            at = (x * ny + y) * share
            weight_ref[at : at + share, :] = arrived_ref[rank, local:, :].astype(F32) * scale


def last_sums(arrived, local, weight_shape, node_total, sizes):
    _, nx, ny = sizes
    return pl.pallas_call(
        functools.partial(last_sums_kernel, nx, ny, 1.0 / math.sqrt(node_total)),
        out_shape=(
            jax.ShapeDtypeStruct((local, weight_shape[1]), BF16),
            jax.ShapeDtypeStruct(weight_shape, F32),
        ),
        in_specs=[VMEM],
        out_specs=(VMEM,) * 2,
        compiler_params=pltpu.CompilerParams(vmem_limit_bytes=VMEM_LIMIT),
    )(arrived)


def body(sizes, node_features, weight, cotangent, adjacency_blocks, block_coords, block_counts):
    depth, nx, ny = sizes
    together = lax.optimization_barrier
    local, width = node_features.shape
    lanes = width // 2
    node_total = local * nx * ny * depth * 2
    at_x = lax.axis_index("x")
    at_y = lax.axis_index("yh") * 2 + lax.axis_index("yl")
    place = jnp.stack([lax.axis_index("z"), lax.axis_index("c"), at_x, at_y]).astype(jnp.int32)
    count = block_counts.reshape(1)

    def rank(x, y):
        return ((y % ny) // 2 * nx + x % nx) * 2 + y % 2

    def send(value, dx, dy):
        pairs = [(rank(x, y), rank(x + dx, y + dy)) for x in range(nx) for y in range(ny)]
        return lax.ppermute(value, PLANE, pairs)

    def climb(value, dz):
        return lax.ppermute(value, "z", [(i, (i + dz) % depth) for i in range(depth)])

    def swap(value, dz=0, core=True):
        pairs = [(z * 2 + c, (z ^ dz) * 2 + (c ^ int(core))) for z in range(depth) for c in range(2)]
        return lax.ppermute(value, ("z", "c"), pairs)

    with jax.named_scope("gather_features"):
        upright, level = node_features[:, :lanes], node_features[:, lanes:]
        got = together(
            tuple(send(upright, -o, 0) for o in range(1, nx)) + tuple(send(level, 0, -o) for o in range(1, ny))
        )
        upright = jnp.concatenate((upright,) + got[: nx - 1], axis=0)
        level = jnp.concatenate((level,) + got[nx - 1 :], axis=0)
        got = together(
            tuple(send(upright, 0, -o) for o in range(1, ny)) + tuple(send(level, -o, 0) for o in range(1, nx))
        )
        pieces = (upright,) + got[: ny - 1] + (level,) + got[ny - 1 :]

    with jax.named_scope("tables"):
        table = slot_tables(block_coords[0, 0], count, place, sizes)
        table, early = together((table, count))
        blocks, _ = hold_blocks(adjacency_blocks[0, 0], early)

    with jax.named_scope("forward"):
        for_sibling, source = sibling_rows(table, blocks, pieces, sizes)
        sibling = swap(for_sibling)
        own = own_rows(0, table, blocks, source, depth)
        sibling, own = together((sibling, own))
        sibling = sibling.reshape(depth, local, width)

    def term(mine, spot):
        return mine.astype(F32) + sibling[spot].astype(F32)

    with jax.named_scope("sum_rows"):
        half = local // 2
        middle = depth // 2
        ends = own.reshape(2, local, width)
        far = term(ends[0], 0).astype(BF16)
        up, down = far[:half], far[half:]
        for step in range(1, middle + 1):
            pace, up, down = together((table, up, down))
            if step < middle:
                mine = own_rows(step, pace, blocks, source, depth).reshape(2, local, width)
            up, down = together((climb(up, 1), climb(down, -1)))
            if step == 1:
                up = jnp.concatenate([up, jnp.zeros_like(up)], axis=0)
                down = jnp.concatenate([jnp.zeros_like(down), down], axis=0)
            if step < middle:
                up = (term(mine[0], 2 * step) + up.astype(F32)).astype(BF16)
                down = (term(mine[1], 2 * step + 1) + down.astype(F32)).astype(BF16)
            else:
                mixed = (term(ends[1], 1) + (up.astype(F32) + down.astype(F32))).astype(BF16)

    with jax.named_scope("dense"):
        hidden, act_grad, mixed_grad = dense(mixed, weight, cotangent)

    with jax.named_scope("gather_rows"):

        chunks = {0: mixed_grad}
        ahead = behind = mixed_grad
        for step in range(1, middle + 1):
            if step < middle:
                moved = (climb(ahead, 1), climb(behind, -1))
            else:
                moved = (climb(ahead[:half], 1), climb(behind[half:], -1))
            if step == 1:
                first, *rest = weight_shares(place, mixed, act_grad, nx)
                terms = [first] + [send(value, d + 1, 0) for d, value in enumerate(rest)]
            elif step <= 3:
                terms = together((tuple(terms), ahead, behind))[0]
                first, *rest = add_cut(place, terms, ny if step == 2 else 1)
                if step == 2:
                    terms = [first] + [send(value, 0, d + 1) for d, value in enumerate(rest)]
                else:
                    terms = [first, swap(first, 1, False)]
            else:
                terms = together((tuple(terms), ahead, behind))[0]
                first = terms[0] + terms[1]
                terms = [first, swap(first, 2, False)]
            ahead, behind, terms[0] = together(moved + (terms[0],))
            if step == 3:
                ahead, behind, *terms = together((ahead, behind, *terms))
            if step < middle:
                chunks[depth - step] = ahead
                chunks[step] = behind
        order = [0] + [d for i in range(1, middle) for d in (middle - i, middle + i)]
        own_panel = own_rows_panel([ahead, behind] + [chunks[d] for d in order])
        own_panel, part = together((own_panel, terms[0] + terms[1]))
        sibling_panel = swap(own_panel)
        part = part + swap(part)
        got = swap(part, 4, False)

    with jax.named_scope("backward"):
        share = part.shape[0]
        outs = backward_product(table, place, blocks, sibling_panel, own_panel, share, sizes)
        outs, got, part = together((outs, got, part))
        tail = jnp.broadcast_to((part + got).astype(BF16)[None], (nx * ny, share, width))
        outs = lax.dynamic_update_slice(outs, tail, (0, local, 0))

    with jax.named_scope("sum_columns"):
        arrived = lax.all_to_all(outs, PLANE, 0, 0, tiled=True)
        feature_grad, weight_grad = last_sums(arrived, local, weight.shape, node_total, sizes)
    return (hidden, weight_grad, feature_grad)


def solution(mesh):
    depth = mesh.shape["row"] // 2
    nx = mesh.shape["col"] // 2
    ny = mesh.shape["rep"] * 2
    fine = Mesh(mesh.devices.reshape(depth, 2, ny // 2, nx, 2), ("z", "c", "yh", "x", "yl"))
    row = ("z", "c")
    in_specs = (
        P((*row, *PLANE), None),
        P(),
        P((*PLANE, *row), None),
        P(PLANE, row, None, None, None),
        P(PLANE, row, None, None),
        P(PLANE, row),
    )
    out_specs = (P((*PLANE, *row), None), P(), P((*row, *PLANE), None))
    return jax.shard_map(
        functools.partial(body, (depth, nx, ny)),
        mesh=fine,
        in_specs=in_specs,
        out_specs=out_specs,
        check_vma=False,
    )
```
